128 devices in a mesh: group: 32 (over x_lo, y, z), tensor: 4 (over x_hi, core).
Axes of the slice: x: 4 (x_hi: 2, x_lo: 2; x = x_hi * 2 + x_lo), y: 4, z: 4, core: 2. Of those that a mesh axis runs over, the one named last changes fastest.
Arguments:
- layer_in: bfloat16 [4, 1024, 4096], P(None, 'group'), may hold values from -6 to 6
- lengths: int32 [1024], P('group'), may hold values from 1 to 4
- prior_state: bfloat16 [1024, 64, 64, 256], P('group', 'tensor'), may hold values from -6 to 6
- weight_x: bfloat16 [4096, 4096], P(('group', 'tensor')), may hold values from -0.09375 to 0.09375
- weight_z: bfloat16 [4096, 4096], P(('group', 'tensor')), may hold values from -0.09375 to 0.09375
- weight_b: bfloat16 [4096, 1024], P(('group', 'tensor')), may hold values from -0.09375 to 0.09375
- weight_c: bfloat16 [4096, 1024], P(('group', 'tensor')), may hold values from -0.09375 to 0.09375
- weight_step: bfloat16 [4096, 64], P(('group', 'tensor')), may hold values from -0.09375 to 0.09375
- weight_out: bfloat16 [4096, 4096], P(None, ('group', 'tensor')), may hold values from -0.09375 to 0.09375
- log_rate: float32 [64], P('tensor'), may hold values from -1 to 1.5
- step_bias: float32 [64], P('tensor'), may hold values from -4 to -1
- skip_gain: float32 [64], P('tensor'), may hold values from 1 to 4
- norm_gain: float32 [4096], P('tensor'), may hold values from 0.1 to 1.9
Outputs:
- layer_out: bfloat16 [4, 1024, 4096], P(None, 'group', 'tensor')
The draws below stay inside these ranges and needn't reach their ends.
All inputs are finite; a program needn't handle non-finite values.
Results may differ from the reference program's by a relative error of at most 0.0033.
Values may be sent and summed in bfloat16 or wider, within the bound.
A program may use at most 128 MiB of HBM per device.

```python
import jax
import jax.numpy as jnp
from jax import lax

D = 4096
P_SIZE = 64
N = 256
HEADS_DEV = 16
STEPS = 4
ROWS = 32
HEADS = 64
ROWS_ALL = 1024
N_TENSOR = 4


def touch_ends(entries, rng, smallest, top_value):
    index_at = [jax.random.randint(jax.random.fold_in(rng, axis), (), 0, length) for axis, length in enumerate(entries.shape)]
    main_axis = entries.shape.index(max(entries.shape))
    next_to = index_at[:main_axis] + [(index_at[main_axis] + 1) % entries.shape[main_axis]] + index_at[main_axis + 1:]
    return entries.at[tuple(index_at)].set(smallest).at[tuple(next_to)].set(top_value)


def levels(stream_key, dims, split, smallest, high):
    level, own = 1.0, jax.random.fold_in(stream_key, 6)
    for axis_at, shards_of in split:
        steps = jnp.exp(jax.random.uniform(jax.random.fold_in(own, axis_at), (shards_of,), jnp.float32, smallest / len(split), high / len(split)))
        level = level * jnp.repeat(steps, dims[axis_at] // shards_of).reshape([-1 if axis == axis_at else 1 for axis in range(len(dims))])
    return level


def noise(stream_key, extent, width, bound, pieces=(), kind=jnp.bfloat16):
    drawn = jax.random.normal(stream_key, extent, jnp.float32) * width
    if len(pieces) > 0:
        drawn = levels(stream_key, extent, pieces, -0.22, 0.18) * drawn
    return jnp.clip(drawn, min=-bound, max=bound).astype(kind)


def setup_inputs(seed: int = 0) -> dict:
    streams_of = jax.random.split(jax.random.key(seed), 14)
    layer_in = noise(streams_of[0], (STEPS, ROWS_ALL, D), 1.0, 6.0, ((1, 32),))
    lengths = touch_ends(jax.random.randint(streams_of[1], (ROWS_ALL,), 1, STEPS + 1), jax.random.fold_in(streams_of[1], 1), 1, STEPS).astype(jnp.int32)
    prior_state = noise(streams_of[2], (ROWS_ALL, HEADS, P_SIZE, N), 1.0, 6.0, ((0, 32), (1, 4)))
    weight_x = noise(streams_of[3], (D, HEADS * P_SIZE), D ** -0.5, 0.09375, ((0, 128),))
    weight_z = noise(streams_of[4], (D, HEADS * P_SIZE), D ** -0.5, 0.09375, ((0, 128),))
    weight_b = noise(streams_of[5], (D, N_TENSOR * N), D ** -0.5, 0.09375, ((0, 128),))
    weight_c = noise(streams_of[6], (D, N_TENSOR * N), D ** -0.5, 0.09375, ((0, 128),))
    weight_step = noise(streams_of[7], (D, HEADS), D ** -0.5, 0.09375, ((0, 128),))
    weight_out = noise(streams_of[8], (HEADS * P_SIZE, D), (HEADS * P_SIZE) ** -0.5, 0.09375, ((1, 128),))
    log_rate = jnp.clip(-1.0 + 2.5 * jax.random.uniform(streams_of[9], (HEADS,), jnp.float32) ** levels(streams_of[9], (HEADS,), ((0, 4),), -0.2, 0.2), -1.0, 1.5)
    step_bias = jnp.clip(-4.0 + 3.0 * jax.random.uniform(streams_of[10], (HEADS,), jnp.float32) ** levels(streams_of[10], (HEADS,), ((0, 4),), -0.2, 0.2), -4.0, -1.0)
    skip_gain = jnp.clip(1.0 + 3.0 * jax.random.uniform(streams_of[11], (HEADS,), jnp.float32) ** levels(streams_of[11], (HEADS,), ((0, 4),), -0.2, 0.2), 1.0, 4.0)
    norm_gain = jnp.clip(1.0 + 0.18 * jax.random.normal(streams_of[12], (HEADS * P_SIZE,), jnp.float32), 0.1, 1.9)
    return dict(layer_in=layer_in, lengths=lengths, prior_state=prior_state, weight_x=weight_x, weight_z=weight_z, weight_b=weight_b, weight_c=weight_c, weight_step=weight_step, weight_out=weight_out, log_rate=log_rate, step_bias=step_bias, skip_gain=skip_gain, norm_gain=norm_gain)


eps = 1e-05

def reference(layer_in, lengths, prior_state, weight_x, weight_z, weight_b, weight_c, weight_step, weight_out, log_rate, step_bias, skip_gain, norm_gain):
    rows_all = layer_in.shape[1]
    block_count = rows_all // ROWS
    base_rate = jnp.exp(log_rate)

    def project(flat_in, weight):
        return jnp.dot(flat_in, weight, preferred_element_type=jnp.float32).reshape(STEPS, ROWS, weight.shape[1])

    def one_block(block_index):
        row_start = (block_index * ROWS).astype(jnp.int32)
        block_in = lax.dynamic_slice_in_dim(layer_in, row_start, ROWS, 1)
        block_len = lax.dynamic_slice_in_dim(lengths, row_start, ROWS, 0)
        carried = lax.dynamic_slice_in_dim(prior_state, row_start, ROWS, 0).astype(jnp.float32)
        flat_in = block_in.reshape(STEPS * ROWS, D)
        x_all = project(flat_in, weight_x)
        z_all = project(flat_in, weight_z)
        b_all = jnp.repeat(project(flat_in, weight_b).reshape(STEPS, ROWS, N_TENSOR, N), HEADS_DEV, axis=2)
        c_all = jnp.repeat(project(flat_in, weight_c).reshape(STEPS, ROWS, N_TENSOR, N), HEADS_DEV, axis=2)
        d_all = project(flat_in, weight_step)
        results = []
        for position in range(STEPS):
            active = block_len > position
            step_size = jax.nn.softplus(d_all[position] + step_bias)
            decay_rate = jnp.exp(-base_rate * step_size)
            x_heads = x_all[position].reshape(ROWS, HEADS, P_SIZE)
            drive_term = (step_size[:, :, None] * x_heads)[..., None] * b_all[position][:, :, None, :]
            updated = decay_rate[:, :, None, None] * carried + drive_term
            carried = jnp.where(active[:, None, None, None], updated, carried)
            mixed_y = jnp.einsum('rhpn,rhn->rhp', carried, c_all[position], precision=lax.Precision.HIGHEST) + skip_gain[:, None] * x_heads
            gated_out = mixed_y.reshape(ROWS, HEADS * P_SIZE) * jax.nn.silu(z_all[position])
            grouped = gated_out.reshape(ROWS, N_TENSOR, HEADS_DEV * P_SIZE)
            inv_rms = lax.rsqrt(lax.optimization_barrier(jnp.mean(grouped * grouped, axis=2, keepdims=True)) + eps)
            hidden = ((grouped * inv_rms).reshape(ROWS, HEADS * P_SIZE) * norm_gain).astype(jnp.bfloat16)
            mix_sum = jnp.dot(hidden, weight_out, preferred_element_type=jnp.float32)
            residual = block_in[position].astype(jnp.float32)
            results.append(jnp.where(active[:, None], residual + mix_sum, residual).astype(jnp.bfloat16))
        return jnp.stack(results)
    blocks_out = lax.map(one_block, jnp.arange(block_count, dtype=jnp.int32))
    return jnp.transpose(blocks_out, (1, 0, 2, 3)).reshape(STEPS, rows_all, D)
```

```python
import jax
import jax.numpy as jnp
from jax import lax
from jax.experimental import pallas as pl
from jax.experimental.pallas import tpu as pltpu
from jax.sharding import PartitionSpec as P

MESH = pl.DeviceIdType.MESH
eps = 1e-05


def here():
    group, tensor = lax.axis_index("group"), lax.axis_index("tensor")
    return (tensor // 2) * 2 + group // 16, (group // 4) % 4, group % 4, tensor % 2


def device(x, y, z, core):
    return ((x % 2) * 16 + (y % 4) * 4 + z % 4, ((x % 4) // 2) * 2 + core % 2)


def remote(source, target, send_sem, recv_sem, where):
    return pltpu.make_async_remote_copy(
        src_ref=source,
        dst_ref=target,
        send_sem=send_sem,
        recv_sem=recv_sem,
        device_id=where,
        device_id_type=MESH,
    )


def arrived(ref, sem):
    pltpu.make_async_copy(ref, ref, sem).wait()


def greet(partners, count):
    barrier = pltpu.get_barrier_semaphore()
    for partner in partners:
        pl.semaphore_signal(barrier, inc=1, device_id=partner, device_id_type=MESH)
    pl.semaphore_wait(barrier, count)


def project_kernel(
    pack_ref,
    fold_ref,
    act_ref,
    xz_ref,
    bc_ref,
    step_ref,
    act,
    weights,
    folded,
    keep,
    give,
    got,
    rounded,
    shared_sum,
    step_give,
    step_got,
    own_sem,
    f_send,
    f_recv,
    g_send,
    g_recv,
    t_sem,
    a_send,
    a_recv,
    b_send,
    b_recv,
    z_send,
    z_recv,
    x_send,
    x_recv,
    d_send,
    d_recv,
    r_send,
    r_recv,
    c_send,
    c_recv,
):
    x, y, z, core = here()
    x_lo, x_hi = x % 2, x // 2
    partners = [
        device(x + dx, y, z + dz, core + dc)
        for dx in range(4)
        for dz in range(4)
        for dc in range(2)
        if (dx, dz, dc) != (0, 0, 0)
    ]
    partners += [device(x, y + 1, z, core), device(x, y + 3, z, core)]
    greet(partners, len(partners))

    row = pl.multiple_of(y * 512 + z * 128 + x_hi * 64 + core * 32, 32)
    landing = weights.at[pl.ds(row, 32)]
    is_self = core == x_lo
    tile_copies = []
    for dz in (2, 1, 3, 0):
        for dx in (2, 1, 3, 0):
            xd, zd = (x + dx) % 4, (z + dz) % 4
            source = pack_ref.at[(xd // 2) * 8 + (xd % 2) * 4 + zd]
            copy = remote(
                source,
                landing,
                a_send.at[dz * 4 + dx],
                a_recv.at[z // 2],
                device(xd, y, zd, x_lo),
            )
            if (dx, dz) == (0, 0):
                local = pltpu.make_async_copy(source, landing, a_recv.at[z // 2])
                pl.when(is_self)(local.start)
                pl.when(jnp.logical_not(is_self))(copy.start)
            else:
                copy.start()
            tile_copies.append(copy)

    fold_row = pl.multiple_of(y * 256 + z * 64 + x_hi * 32 + core * 16, 16)
    fold_landing = folded.at[pl.ds(fold_row, 16)]
    for dz in (2, 1, 3, 0):
        for dx in (2, 1, 3, 0):
            copy = remote(
                fold_ref,
                fold_landing,
                f_send.at[dz * 4 + dx],
                f_recv.at[0],
                device(x + dx, y, z + dz, x_lo),
            )
            if (dx, dz) == (0, 0):
                local = pltpu.make_async_copy(fold_ref, fold_landing, f_recv.at[0])
                pl.when(is_self)(local.start)
                pl.when(jnp.logical_not(is_self))(copy.start)
            else:
                copy.start()
            tile_copies.append(copy)

    half = pl.ds(pl.multiple_of(core * 2048, 2048), 2048)
    mine = x_lo * 4 + z

    def piece(dz, h):
        return act.at[x_lo * 4 + (z + dz) % 4, pl.ds(h * 64, 64)]

    own_copy = pltpu.make_async_copy(act_ref.at[:, half], act.at[mine], own_sem)
    own_copy.start()
    started = []

    def z_go(source, target, slot, step):
        copy = remote(
            source, target, z_send.at[slot], z_recv.at[slot], device(x, y, z + step, core)
        )
        copy.start()
        started.append(copy)

    def x_go(source, target, rel, h):
        slot = rel * 2 + h
        copy = remote(
            source,
            target,
            x_send.at[slot],
            x_recv.at[slot],
            device(x + (1 if h == 0 else 3), y, z, core),
        )
        copy.start()
        started.append(copy)

    own_half = [act_ref.at[pl.ds(h * 64, 64), half] for h in range(2)]
    z_go(own_half[0], piece(0, 0), 0, 1)
    z_go(own_half[1], piece(0, 1), 3, 3)
    x_go(own_half[0], piece(0, 0), 0, 0)
    x_go(own_half[1], piece(0, 1), 0, 1)
    z_go(own_half[1], piece(0, 1), 1, 1)
    z_go(own_half[0], piece(0, 0), 2, 3)

    def block(dy, h):
        return weights.at[pl.ds(pl.multiple_of(((y + dy) % 4) * 512 + h * 256, 256), 256)]

    def y_go(dy, h, slot, step):
        copy = remote(
            block(dy, h),
            block(dy, h),
            b_send.at[slot],
            b_recv.at[slot],
            device(x, y + step, z, core),
        )
        copy.start()
        started.append(copy)

    def fold(dy, h):
        return folded.at[pl.ds(pl.multiple_of(((y + dy) % 4) * 256 + h * 128, 128), 128)]

    def f_go(dy, h, slot, step):
        copy = remote(
            fold(dy, h),
            fold(dy, h),
            g_send.at[slot],
            g_recv.at[slot],
            device(x, y + step, z, core),
        )
        copy.start()
        started.append(copy)

    arrived(block(0, 0), a_recv.at[0])
    y_go(0, 0, 0, 1)
    arrived(block(0, 1), a_recv.at[1])
    y_go(0, 1, 3, 3)
    y_go(0, 1, 1, 1)
    y_go(0, 0, 2, 3)
    arrived(folded.at[pl.ds(pl.multiple_of(y * 256, 256), 256)], f_recv.at[0])
    f_go(0, 0, 0, 1)
    f_go(0, 1, 3, 3)
    f_go(0, 1, 1, 1)
    f_go(0, 0, 2, 3)

    arrived(piece(3, 0), z_recv.at[0])
    z_go(piece(3, 0), piece(3, 0), 4, 1)
    x_go(piece(3, 0), piece(3, 0), 1, 0)
    arrived(piece(1, 1), z_recv.at[3])
    z_go(piece(1, 1), piece(1, 1), 5, 3)
    x_go(piece(1, 1), piece(1, 1), 2, 1)
    arrived(piece(3, 1), z_recv.at[1])
    x_go(piece(3, 1), piece(3, 1), 1, 1)
    arrived(piece(1, 0), z_recv.at[2])
    x_go(piece(1, 0), piece(1, 0), 2, 0)

    arrived(block(3, 0), b_recv.at[0])
    y_go(3, 0, 4, 1)
    arrived(block(1, 1), b_recv.at[3])
    y_go(1, 1, 5, 3)
    arrived(fold(3, 0), g_recv.at[0])
    f_go(3, 0, 4, 1)
    arrived(fold(1, 1), g_recv.at[3])
    f_go(1, 1, 5, 3)

    arrived(piece(2, 0), z_recv.at[4])
    x_go(piece(2, 0), piece(2, 0), 3, 0)
    arrived(piece(2, 1), z_recv.at[5])
    x_go(piece(2, 1), piece(2, 1), 3, 1)

    def other(dz, h):
        return act.at[(1 - x_lo) * 4 + (z + dz) % 4, pl.ds(h * 64, 64)]

    for rel, dz in enumerate((0, 3, 1, 2)):
        for h in range(2):
            arrived(other(dz, h), x_recv.at[rel * 2 + h])
    own_copy.wait()
    arrived(block(3, 1), b_recv.at[1])
    arrived(block(1, 0), b_recv.at[2])
    arrived(block(2, 0), b_recv.at[4])
    arrived(block(2, 1), b_recv.at[5])
    arrived(fold(3, 1), g_recv.at[1])
    arrived(fold(1, 0), g_recv.at[2])
    arrived(fold(2, 0), g_recv.at[4])
    arrived(fold(2, 1), g_recv.at[5])

    def to_twin(i):
        return remote(
            give.at[i], got.at[i], d_send.at[i], d_recv.at[i], device(x, y, z, core + 1)
        )

    def multiply(i, carry):
        product = jnp.dot(act[i], weights[...], preferred_element_type=jnp.float32)
        first, second, shared = product[:, :256], product[:, 256:512], product[:, 512:]
        keep[i, :, :256] = jnp.where(core == 0, first, second)
        keep[i, :, 256:] = shared
        give[i, :, :256] = jnp.where(core == 0, second, first)
        give[i, :, 256:] = shared
        to_twin(i).start()
        return carry

    lax.fori_loop(0, 8, multiply, 0)

    pairs = folded[...].reshape(64, 16, 128)
    step_weight = jnp.concatenate([pairs[:, :, :64], pairs[:, :, 64:]], axis=1).reshape(2048, 64)
    step_half = jnp.dot(act[mine], step_weight, preferred_element_type=jnp.float32)
    step_give[...] = jnp.concatenate([step_half, step_half], axis=1)
    step_copy = remote(
        step_give, step_got, t_sem.at[0], t_sem.at[1], device(x, y, z, core + 1)
    )
    step_copy.start()

    bc_slot = x_lo * 2 + z % 2
    has_bc = core == z // 2

    def xz_copies(i):
        source, target = rounded.at[i], xz_ref.at[mine]
        where = device(x_hi * 2 + i // 4, y, i % 4, core)
        return (
            remote(source, target, r_send.at[i], r_recv.at[mine], where),
            pltpu.make_async_copy(source, target, r_recv.at[mine]),
        )

    def bc_copies(i):
        source, target = shared_sum.at[i], bc_ref.at[bc_slot]
        where = device(x_hi * 2 + i // 4, y, i % 4, core)
        return (
            remote(source, target, c_send.at[i], c_recv.at[bc_slot], where),
            pltpu.make_async_copy(source, target, c_recv.at[bc_slot]),
        )

    def hand_out(i, carry):
        copy = to_twin(i)
        copy.wait_recv()
        total = keep[i] + got[i]
        gate = total[:, 128:256]
        rounded[i, :, :128] = total[:, :128].astype(jnp.bfloat16)
        rounded[i, :, 128:] = (gate / (1.0 + jnp.exp(-gate))).astype(jnp.bfloat16)
        shared_sum[i] = total[:, 256:]
        far, near = xz_copies(i)
        pl.when(i != mine)(far.start)
        pl.when(i == mine)(near.start)
        far, near = bc_copies(i)
        pl.when(jnp.logical_and(has_bc, i != mine))(far.start)
        pl.when(jnp.logical_and(has_bc, i == mine))(near.start)
        return carry

    lax.fori_loop(0, 8, hand_out, 0)

    def finish(i, carry):
        to_twin(i).wait_send()
        pl.when(i != mine)(xz_copies(i)[0].wait_send)
        pl.when(jnp.logical_and(has_bc, i != mine))(bc_copies(i)[0].wait_send)
        arrived(xz_ref.at[i], r_recv.at[i])
        return carry

    lax.fori_loop(0, 8, finish, 0)
    step_copy.wait()
    step_sum = step_give[...] + step_got[...]
    columns = jnp.zeros((128, 16), jnp.float32)
    for t in range(4):
        columns += jnp.where(x_hi * 2 + core == t, step_sum[:, t * 16 : t * 16 + 16], 0.0)
    step_ref[...] = columns
    for slot in range(4):
        arrived(bc_ref.at[slot], c_recv.at[slot])
    for copy in started:
        copy.wait_send()
    for n, copy in enumerate(tile_copies):
        if n % 16 == 15:
            pl.when(jnp.logical_not(is_self))(copy.wait_send)
        else:
            copy.wait_send()


def project(pack, fold, flat_in):
    dma = pltpu.SemaphoreType.DMA
    return pl.pallas_call(
        project_kernel,
        out_shape=(
            jax.ShapeDtypeStruct((8, 128, 256), jnp.bfloat16),
            jax.ShapeDtypeStruct((4, 128, 128), jnp.float32),
            jax.ShapeDtypeStruct((128, 16), jnp.float32),
        ),
        in_specs=[pl.BlockSpec(memory_space=pltpu.VMEM)] * 3,
        out_specs=(pl.BlockSpec(memory_space=pltpu.VMEM),) * 3,
        scratch_shapes=[
            pltpu.VMEM((8, 128, 2048), jnp.bfloat16),
            pltpu.VMEM((2048, 640), jnp.bfloat16),
            pltpu.VMEM((1024, 128), jnp.bfloat16),
            pltpu.VMEM((8, 128, 384), jnp.float32),
            pltpu.VMEM((8, 128, 384), jnp.float32),
            pltpu.VMEM((8, 128, 384), jnp.float32),
            pltpu.VMEM((8, 128, 256), jnp.bfloat16),
            pltpu.VMEM((8, 128, 128), jnp.float32),
            pltpu.VMEM((128, 128), jnp.float32),
            pltpu.VMEM((128, 128), jnp.float32),
            dma(()),
            dma((16,)),
            dma((1,)),
            dma((6,)),
            dma((6,)),
            dma((2,)),
            dma((16,)),
            dma((2,)),
            dma((6,)),
            dma((6,)),
            dma((6,)),
            dma((6,)),
            dma((8,)),
            dma((8,)),
            dma((8,)),
            dma((8,)),
            dma((8,)),
            dma((8,)),
            dma((8,)),
            dma((4,)),
        ],
        compiler_params=pltpu.CompilerParams(
            collective_id=0, has_side_effects=True, vmem_limit_bytes=32 << 20
        ),
        cost_estimate=pl.CostEstimate(
            flops=1024 * 2048 * 640 * 2, bytes_accessed=150 << 20, transcendentals=0
        ),
        name="project",
    )(pack, fold, flat_in)


def mixer_kernel(
    xz_ref, bc_ref, step_ref, rate_ref, bias_ref, skip_ref, gain_ref, state_ref, hidden_ref, read, late
):
    spot = pl.program_id(0)

    @pl.when(spot == 0)
    def _():
        late[0] = bc_ref[2]
        late[1] = bc_ref[3]

    for at in range(4):
        row = spot * 4 + at
        steps_of = pl.ds(row, 4, stride=32)
        c_rows = jnp.concatenate([late[0, steps_of, :], late[1, steps_of, :]], axis=1)
        upper = c_rows.astype(jnp.bfloat16)
        lower = (c_rows - upper.astype(jnp.float32)).astype(jnp.bfloat16)
        seen = lax.dot_general(
            jnp.concatenate([upper, lower], axis=0),
            state_ref[at],
            (((1,), (1,)), ((), ())),
            preferred_element_type=jnp.float32,
        )
        for t in range(4):
            read[pl.ds(t * 32 + row, 1), :] = seen[t : t + 1] + seen[t + 4 : t + 5]

    @pl.when(spot == 7)
    def _():
        raw = step_ref[...] + bias_ref[...]
        step = jnp.maximum(raw, 0.0) + jnp.log1p(jnp.exp(-jnp.abs(raw)))
        decay = jnp.exp(-jnp.exp(rate_ref[...]) * step)
        at = [slice(t * 32, t * 32 + 32) for t in range(4)]
        b = jnp.concatenate([bc_ref[0], bc_ref[1]], axis=1)
        c = jnp.concatenate([late[0], late[1]], axis=1)
        rows, total, coefs = [], None, []
        for t in range(4):
            total = decay[at[t]] if t == 0 else total * decay[at[t]]
            coefs = [member * decay[at[t]] for member in coefs] + [step[at[t]]]
            rows.append(total)
            for s in range(t + 1):
                weight = jnp.sum(b[at[s]] * c[at[t]], axis=1, keepdims=True)
                term = coefs[s] * weight
                rows.append(term + skip_ref[...] if s == t else term)
        table = jnp.concatenate(rows, axis=0)
        head = lax.broadcasted_iota(jnp.int32, (16, 1024), 0)
        channel = lax.broadcasted_iota(jnp.int32, (16, 1024), 1)
        spread = jnp.where(channel // 64 == head, 1.0, 0.0).astype(jnp.float32)
        wide = jnp.dot(
            table, spread, precision=lax.Precision.HIGHEST, preferred_element_type=jnp.float32
        )
        xs = [
            jnp.concatenate([xz_ref[j, at[t], :128] for j in range(8)], axis=1).astype(jnp.float32)
            for t in range(4)
        ]
        k = 0
        for t in range(4):
            y = wide[k * 32 : k * 32 + 32] * read[at[t], :]
            k += 1
            for s in range(t + 1):
                y += wide[k * 32 : k * 32 + 32] * xs[s]
                k += 1
            gate = jnp.concatenate([xz_ref[j, at[t], 128:] for j in range(8)], axis=1)
            gated = y * gate.astype(jnp.float32)
            inv_rms = lax.rsqrt(jnp.mean(gated * gated, axis=1, keepdims=True) + eps)
            hidden_ref[at[t], :] = (gated * inv_rms * gain_ref[...]).astype(jnp.bfloat16)


def mixer(xz, bc, step_raw, log_rate, step_bias, skip_gain, norm_gain, state):
    whole = lambda shape: pl.BlockSpec(shape, lambda i: (0,) * len(shape))
    return pl.pallas_call(
        mixer_kernel,
        grid=(8,),
        out_shape=jax.ShapeDtypeStruct((128, 1024), jnp.bfloat16),
        in_specs=[
            whole((8, 128, 256)),
            whole((4, 128, 128)),
            whole((128, 16)),
            whole((1, 16)),
            whole((1, 16)),
            whole((1, 16)),
            whole((1, 1024)),
            pl.BlockSpec((4, 1024, 256), lambda i: (i, 0, 0)),
        ],
        out_specs=whole((128, 1024)),
        scratch_shapes=[
            pltpu.VMEM((128, 1024), jnp.float32),
            pltpu.VMEM((2, 128, 128), jnp.float32),
        ],
        compiler_params=pltpu.CompilerParams(vmem_limit_bytes=32 << 20),
        cost_estimate=pl.CostEstimate(
            flops=32 * 1024 * 256 * 8, bytes_accessed=18 << 20, transcendentals=1 << 18
        ),
        name="mixer",
    )(
        xz,
        bc,
        step_raw,
        log_rate.reshape(1, 16),
        step_bias.reshape(1, 16),
        skip_gain.reshape(1, 16),
        norm_gain.reshape(1, 1024),
        state,
    )


def output_kernel(
    hidden_ref,
    out_weight_ref,
    mix_ref,
    hid,
    weights,
    keep,
    give,
    got,
    rounded,
    own_sem,
    w_send,
    w_recv,
    s1_send,
    s1_recv,
    s2_send,
    s2_recv,
    d_send,
    d_recv,
    r_send,
    r_recv,
):
    x, y, z, core = here()
    x_lo, x_hi = x % 2, x // 2
    mine = x_lo * 4 + z
    target_x = x_lo * 2 + y % 2

    barrier = pltpu.get_barrier_semaphore()

    def signal(where):
        pl.semaphore_signal(barrier, inc=1, device_id=where, device_id_type=MESH)

    self_chip = target_x == x
    for hi in range(2):
        for up in range(2):
            for dc in range(2):
                xs, ys, cs = hi * 2 + x_hi, up * 2 + x_lo, dc
                same = jnp.logical_and(
                    jnp.logical_and(xs == x, ys == y), cs == core
                )
                pl.when(jnp.logical_not(same))(lambda w=device(xs, ys, z, cs): signal(w))
    for step in (1, 2, 3):
        signal(device(x + step, y, z, core))
        signal(device(x, y, z + step, core))
    for step in range(1, 8):
        other = (mine + step) % 8
        signal(device(x_hi * 2 + other // 4, y, other % 4, core))
    signal(device(x, y, z, core + 1))
    expected = 8 + 6 + 7 + 1
    pl.semaphore_wait(barrier, expected - jnp.where(self_chip, 1, 0))

    started = []
    own_copy = pltpu.make_async_copy(hidden_ref, hid.at[x, z], own_sem)
    own_copy.start()

    def part(h, dx, dz):
        return hid.at[(x + dx) % 4, (z + dz) % 4, pl.ds(h * 64, 64)]

    turns = (1, 3, 2)

    def go(h, source, target, stage, slot, step, along_x):
        send, recv = (s1_send, s1_recv) if stage == 1 else (s2_send, s2_recv)
        where = device(x + step, y, z, core) if along_x else device(x, y, z + step, core)
        copy = remote(source, target, send.at[h, slot], recv.at[h, slot], where)
        copy.start()
        started.append(copy)

    for n, step in enumerate(turns):
        for h in range(2):
            source = hidden_ref.at[pl.ds(h * 64, 64)]
            go(h, source, part(h, 0, 0), 1, n, step, h == 1)
    for n, step in enumerate(turns):
        for h in range(2):
            source = hidden_ref.at[pl.ds(h * 64, 64)]
            go(h, source, part(h, 0, 0), 2, n, step, h == 0)

    rows = pl.ds(pl.multiple_of((y // 2) * 128 + (x_hi * 2 + core) * 32, 32), 32)
    weight_copies = []
    for dy in (1, 2, 3, 0):
        for dc in (1, 0):
            cd = (core + dc) % 2
            slot = dy * 2 + dc
            copy = remote(
                out_weight_ref.at[cd],
                weights.at[rows],
                w_send.at[slot],
                w_recv.at[0],
                device(target_x, y + dy, z, cd),
            )
            if (dy, dc) == (0, 0):
                local = pltpu.make_async_copy(
                    out_weight_ref.at[cd], weights.at[rows], w_recv.at[0]
                )
                pl.when(self_chip)(local.start)
                pl.when(jnp.logical_not(self_chip))(copy.start)
            else:
                copy.start()
            weight_copies.append(copy)

    for n, step in enumerate(turns):
        for h in range(2):
            back = (4 - step) % 4
            held = part(h, 0, back) if h == 0 else part(h, back, 0)
            arrived(held, s1_recv.at[h, n])
            for m, onward in enumerate(turns):
                go(h, held, held, 2, 3 + n * 3 + m, onward, h == 0)

    for h in range(2):
        for n, back in enumerate((0, 3, 1, 2)):
            for m, step in enumerate(turns):
                away = (4 - step) % 4
                held = part(h, away, back) if h == 0 else part(h, back, away)
                arrived(held, s2_recv.at[h, n * 3 + m])
    own_copy.wait()
    arrived(weights, w_recv.at[0])

    def to_twin(i):
        return remote(
            give.at[i], got.at[i], d_send.at[i], d_recv.at[i], device(x, y, z, core + 1)
        )

    def against(left, right):
        return lax.dot_general(
            left, right, (((1,), (1,)), ((), ())), preferred_element_type=jnp.float32
        )

    def multiply(i, carry):
        product = against(hid[i // 4, i % 4], weights[:, :1024]) + against(
            hid[2 + i // 4, i % 4], weights[:, 1024:]
        )
        first, second = product[:, :128], product[:, 128:]
        keep[i] = jnp.where(core == 0, first, second)
        give[i] = jnp.where(core == 0, second, first)
        to_twin(i).start()
        return carry

    lax.fori_loop(0, 8, multiply, 0)

    lanes = pl.ds(pl.multiple_of(mine * 128, 128), 128)

    def mix_copies(i):
        where = device(x_hi * 2 + i // 4, y, i % 4, core)
        return (
            remote(rounded.at[i], mix_ref.at[:, lanes], r_send.at[i], r_recv.at[mine], where),
            pltpu.make_async_copy(rounded.at[i], mix_ref.at[:, lanes], r_recv.at[mine]),
        )

    def hand_out(i, carry):
        to_twin(i).wait_recv()
        rounded[i] = keep[i] + got[i]
        far, near = mix_copies(i)
        pl.when(i != mine)(far.start)
        pl.when(i == mine)(near.start)
        return carry

    lax.fori_loop(0, 8, hand_out, 0)

    def finish(i, carry):
        to_twin(i).wait_send()
        pl.when(i != mine)(mix_copies(i)[0].wait_send)
        arrived(mix_ref.at[:, pl.ds(pl.multiple_of(i * 128, 128), 128)], r_recv.at[i])
        return carry

    lax.fori_loop(0, 8, finish, 0)
    for copy in started:
        copy.wait_send()
    for copy in weight_copies[:-1]:
        copy.wait_send()
    pl.when(jnp.logical_not(self_chip))(weight_copies[-1].wait_send)


def output(hidden, out_weight):
    dma = pltpu.SemaphoreType.DMA
    return pl.pallas_call(
        output_kernel,
        out_shape=jax.ShapeDtypeStruct((128, 1024), jnp.float32),
        in_specs=[pl.BlockSpec(memory_space=pltpu.VMEM)] * 2,
        out_specs=pl.BlockSpec(memory_space=pltpu.VMEM),
        scratch_shapes=[
            pltpu.VMEM((4, 4, 128, 1024), jnp.bfloat16),
            pltpu.VMEM((256, 2048), jnp.bfloat16),
            pltpu.VMEM((8, 128, 128), jnp.float32),
            pltpu.VMEM((8, 128, 128), jnp.float32),
            pltpu.VMEM((8, 128, 128), jnp.float32),
            pltpu.VMEM((8, 128, 128), jnp.float32),
            dma(()),
            dma((8,)),
            dma((1,)),
            dma((2, 3)),
            dma((2, 3)),
            dma((2, 12)),
            dma((2, 12)),
            dma((8,)),
            dma((8,)),
            dma((8,)),
            dma((8,)),
        ],
        compiler_params=pltpu.CompilerParams(
            collective_id=1, has_side_effects=True, vmem_limit_bytes=32 << 20
        ),
        cost_estimate=pl.CostEstimate(
            flops=1024 * 2048 * 256 * 2, bytes_accessed=100 << 20, transcendentals=0
        ),
        name="output",
    )(hidden, out_weight)


def shards(
    layer_in,
    lengths,
    prior_state,
    weight_x,
    weight_z,
    weight_b,
    weight_c,
    weight_step,
    weight_out,
    log_rate,
    step_bias,
    skip_gain,
    norm_gain,
):
    tensor = lax.axis_index("tensor")
    flat_in = layer_in.reshape(128, 4096)

    def by_chip(weight):
        return weight.reshape(32, 2, 2, 8, 128).transpose(1, 3, 0, 2, 4)

    def by_row(weight):
        return weight.reshape(32, 2, 4, 128).transpose(1, 2, 0, 3)

    pair = jnp.stack([by_chip(weight_x), by_chip(weight_z)], axis=4).reshape(16, 32, 512)
    shared = jnp.concatenate([by_row(weight_b), by_row(weight_c)], axis=1).reshape(16, 32, 128)
    pack = jnp.concatenate([pair, shared], axis=2)
    fold = jnp.concatenate([weight_step[:16], weight_step[16:]], axis=1)
    xz, bc, step_raw = project(pack, fold, flat_in)
    hidden = mixer(
        xz,
        bc,
        step_raw,
        log_rate,
        step_bias,
        skip_gain,
        norm_gain,
        prior_state.reshape(32, 1024, 256),
    )

    out_weight = (
        weight_out.T.reshape(32, 2, 2, 1024).transpose(2, 0, 1, 3).reshape(2, 32, 2048)
    )
    mix = output(hidden, out_weight).reshape(4, 32, 1024)
    residual = lax.dynamic_slice_in_dim(layer_in, tensor * 1024, 1024, 2).astype(jnp.float32)
    active = lengths[None, :] > jnp.arange(4, dtype=jnp.int32)[:, None]
    return jnp.where(active[:, :, None], residual + mix, residual).astype(jnp.bfloat16)


def solution(mesh):
    placed = (
        P(None, "group", None),
        P("group"),
        P("group", "tensor", None, None),
        P(("group", "tensor"), None),
        P(("group", "tensor"), None),
        P(("group", "tensor"), None),
        P(("group", "tensor"), None),
        P(("group", "tensor"), None),
        P(None, ("group", "tensor")),
        P("tensor"),
        P("tensor"),
        P("tensor"),
        P("tensor"),
    )
    return jax.shard_map(
        shards, mesh=mesh, in_specs=placed, out_specs=P(None, "group", "tensor"), check_vma=False
    )
```

```python
import jax
import jax.numpy as jnp
from jax import lax
from jax.experimental import pallas as pl
from jax.experimental.pallas import tpu as pltpu
from jax.sharding import PartitionSpec as P

MESH = pl.DeviceIdType.MESH
eps = 1e-05


def here():
    group, tensor = lax.axis_index("group"), lax.axis_index("tensor")
    return (tensor // 2) * 2 + group // 16, (group // 4) % 4, group % 4, tensor % 2


def device(x, y, z, core):
    return ((x % 2) * 16 + (y % 4) * 4 + z % 4, ((x % 4) // 2) * 2 + core % 2)


def remote(source, target, send_sem, recv_sem, where):
    return pltpu.make_async_remote_copy(
        src_ref=source,
        dst_ref=target,
        send_sem=send_sem,
        recv_sem=recv_sem,
        device_id=where,
        device_id_type=MESH,
    )


def arrived(ref, sem):
    pltpu.make_async_copy(ref, ref, sem).wait()


TURNS = (1, 3, 2)


def mixer_kernel(
    pack_ref,
    act_ref,
    out_weight_ref,
    rate_ref,
    bias_ref,
    skip_ref,
    gain_ref,
    state_ref,
    mix_ref,
    act,
    landed,
    weights,
    step_weights,
    keep,
    give,
    got,
    rounded,
    shared_sum,
    xz,
    bc,
    step_give,
    step_got,
    state,
    read,
    quarter,
    out_weights,
    hid,
    out_keep,
    out_give,
    out_got,
    back,
    s_sem,
    a_send,
    a_recv,
    b_send,
    b_recv,
    z_send,
    z_recv,
    x_send,
    x_recv,
    d_send,
    d_recv,
    r_send,
    r_recv,
    c_send,
    c_recv,
    t_sem,
    q_sem,
    w_sem,
    o1_send,
    o1_recv,
    o2_send,
    o2_recv,
    h_send,
    h_recv,
    e_send,
    e_recv,
    f_sem,
):
    x, y, z, core = here()
    x_lo, x_hi = x % 2, x // 2
    mine = x_lo * 4 + z
    twin = device(x, y, z, core + 1)
    started = []

    target_x, target_y = x_lo * 2 + y % 2, y + x_hi
    stays = jnp.logical_and(target_x == x, x_hi == 0)
    k_here = (y - x_lo + 4) % 4
    source = device((k_here % 2) * 2 + x_hi, (k_here // 2) * 2 + x_lo, z, core)

    barrier = pltpu.get_barrier_semaphore()

    def signal(where):
        pl.semaphore_signal(barrier, inc=1, device_id=where, device_id_type=MESH)

    plane = [(dx, dz) for dz in (2, 1, 3, 0) for dx in (2, 1, 3, 0)]
    for dx, dz in plane[:-1]:
        signal(device(x + dx, y, z + dz, core))
    for step in TURNS:
        signal(device(x, y + step, z, core))
    signal(twin)
    pl.when(jnp.logical_not(stays))(lambda: signal(source))

    lane = lax.broadcasted_iota(jnp.int32, (256, 128), 1)
    from_lane = lax.broadcasted_iota(jnp.int32, (256, 128), 0)
    chosen = from_lane == (lane // 32) * 64 + core * 32 + lane % 32
    picker = jnp.where(chosen, 1.0, 0.0).astype(jnp.bfloat16)
    for i in range(16):
        spot = ((i % 8) // 2) * 4 + (i // 8) * 2 + i % 2
        act[mine, :, spot * 128 : spot * 128 + 128] = jnp.dot(
            act_ref[:, i * 256 : i * 256 + 256], picker, preferred_element_type=jnp.float32
        ).astype(jnp.bfloat16)

    pl.semaphore_wait(barrier, 20 - jnp.where(stays, 1, 0))

    landing = landed.at[y, x_lo * 8 + z * 2 + x_hi]
    for n, (dx, dz) in enumerate(plane):
        xd, zd = (x + dx) % 4, (z + dz) % 4
        tile = pack_ref.at[(xd // 2) * 8 + (xd % 2) * 4 + zd]
        if n == 15:
            pltpu.make_async_copy(tile, landing, a_recv.at[x_lo]).start()
        else:
            copy = remote(tile, landing, a_send.at[n], a_recv.at[x_lo], device(xd, y, zd, core))
            copy.start()
            started.append(copy)

    def piece(dz, h):
        return act.at[x_lo * 4 + (z + dz) % 4, pl.ds(h * 64, 64)]

    def z_go(dz, h, slot, step):
        copy = remote(
            piece(dz, h),
            piece(dz, h),
            z_send.at[slot],
            z_recv.at[slot],
            device(x, y, z + step, core),
        )
        copy.start()
        started.append(copy)

    def x_go(dz, h, rel):
        slot = rel * 2 + h
        copy = remote(
            piece(dz, h),
            piece(dz, h),
            x_send.at[slot],
            x_recv.at[slot],
            device(x + (1 if h == 0 else 3), y, z, core),
        )
        copy.start()
        started.append(copy)

    z_go(0, 0, 0, 1)
    z_go(0, 1, 3, 3)
    x_go(0, 0, 0)
    x_go(0, 1, 0)
    z_go(0, 1, 1, 1)
    z_go(0, 0, 2, 3)

    quarter_copy = remote(
        out_weight_ref.at[1 - core], quarter.at[core], q_sem.at[0], q_sem.at[1], twin
    )
    quarter_copy.start()
    started.append(quarter_copy)
    quarter_own = pltpu.make_async_copy(
        out_weight_ref.at[core], quarter.at[core], q_sem.at[2]
    )
    quarter_own.start()

    state_copies = [
        pltpu.make_async_copy(
            state_ref.at[pl.ds(n * 8, 8)], state.at[pl.ds(n * 8, 8)], s_sem.at[n]
        )
        for n in range(4)
    ]
    for copy in state_copies:
        copy.start()

    def block(dy, h):
        return landed.at[(y + dy) % 4, pl.ds(h * 8, 8)]

    def y_go(dy, h, slot, step):
        copy = remote(
            block(dy, h),
            block(dy, h),
            b_send.at[slot],
            b_recv.at[slot],
            device(x, y + step, z, core),
        )
        copy.start()
        started.append(copy)

    def lay_out(dy):
        at = (y + dy) % 4
        rows = pl.ds(pl.multiple_of(at * 512, 512), 512)
        for n in range(5):
            weights[rows, n * 128 : n * 128 + 128] = landed[
                at, :, n * 32 : n * 32 + 32, :
            ].reshape(512, 128)
        pairs = landed[at, :, 160:176, :]
        step_weights[rows, :] = jnp.concatenate(
            [pairs[:, :, :64], pairs[:, :, 64:]], axis=1
        ).reshape(512, 64)

    arrived(block(0, 0), a_recv.at[0])
    y_go(0, 0, 0, 1)
    arrived(block(0, 1), a_recv.at[1])
    y_go(0, 1, 3, 3)
    y_go(0, 1, 1, 1)
    y_go(0, 0, 2, 3)

    quarter_own.wait()
    arrived(quarter.at[1 - core], q_sem.at[1])
    sent_on = remote(
        quarter,
        out_weights.at[y // 2, z, x_hi],
        w_sem.at[0],
        w_sem.at[1],
        device(target_x, target_y, z, core),
    )
    kept = pltpu.make_async_copy(quarter, out_weights.at[y // 2, z, x_hi], w_sem.at[1])
    pl.when(jnp.logical_not(stays))(sent_on.start)
    pl.when(stays)(kept.start)

    arrived(piece(3, 0), z_recv.at[0])
    z_go(3, 0, 4, 1)
    x_go(3, 0, 1)
    arrived(piece(1, 1), z_recv.at[3])
    z_go(1, 1, 5, 3)
    x_go(1, 1, 2)
    lay_out(0)
    arrived(piece(3, 1), z_recv.at[1])
    x_go(3, 1, 1)
    arrived(piece(1, 0), z_recv.at[2])
    x_go(1, 0, 2)

    arrived(block(3, 0), b_recv.at[0])
    y_go(3, 0, 4, 1)
    arrived(block(1, 1), b_recv.at[3])
    y_go(1, 1, 5, 3)

    arrived(piece(2, 0), z_recv.at[4])
    x_go(2, 0, 3)
    arrived(piece(2, 1), z_recv.at[5])
    x_go(2, 1, 3)

    arrived(block(3, 1), b_recv.at[1])
    lay_out(3)
    arrived(block(1, 0), b_recv.at[2])
    lay_out(1)

    def other(dz, h):
        return act.at[(1 - x_lo) * 4 + (z + dz) % 4, pl.ds(h * 64, 64)]

    for rel, dz in enumerate((0, 3, 1, 2)):
        for h in range(2):
            arrived(other(dz, h), x_recv.at[rel * 2 + h])
    arrived(block(2, 0), b_recv.at[4])
    arrived(block(2, 1), b_recv.at[5])
    lay_out(2)

    def columns(dk, dz, h):
        k = (k_here + dk) % 4
        return out_weights.at[k // 2, (z + dz) % 4, k % 2, h]

    def o_go(h, held, stage, slot, step, along_y):
        send, recv = (o1_send, o1_recv) if stage == 1 else (o2_send, o2_recv)
        where = device(x, y + step, z, core) if along_y else device(x, y, z + step, core)
        copy = remote(held, held, send.at[h, slot], recv.at[h, slot], where)
        copy.start()
        started.append(copy)

    arrived(out_weights.at[k_here // 2, z, k_here % 2], w_sem.at[1])
    for n, step in enumerate(TURNS):
        for h in range(2):
            o_go(h, columns(0, 0, h), 1, n, step, h == 1)
    for n, step in enumerate(TURNS):
        for h in range(2):
            o_go(h, columns(0, 0, h), 2, n, step, h == 0)

    def to_twin(i):
        return remote(give.at[i], got.at[i], d_send.at[i], d_recv.at[i], twin)

    step_half = jnp.dot(act[mine], step_weights[...], preferred_element_type=jnp.float32)
    step_give[...] = jnp.concatenate([step_half, step_half], axis=1)
    step_copy = remote(step_give, step_got, t_sem.at[0], t_sem.at[1], twin)
    step_copy.start()

    def multiply(i, carry):
        product = jnp.dot(act[i], weights[...], preferred_element_type=jnp.float32)
        first, second, shared = product[:, :256], product[:, 256:512], product[:, 512:]
        keep[i, :, :256] = jnp.where(core == 0, first, second)
        keep[i, :, 256:] = shared
        give[i, :, :256] = jnp.where(core == 0, second, first)
        give[i, :, 256:] = shared
        to_twin(i).start()
        return carry

    lax.fori_loop(0, 8, multiply, 0)

    bc_slot = x_lo * 2 + z % 2
    has_bc = core == z // 2

    def owner(i):
        return device(x_hi * 2 + i // 4, y, i % 4, core)

    def xz_far(i):
        return remote(rounded.at[i], xz.at[mine], r_send.at[i], r_recv.at[mine], owner(i))

    def bc_far(i):
        return remote(
            shared_sum.at[i], bc.at[bc_slot], c_send.at[i], c_recv.at[bc_slot], owner(i)
        )

    def hand_out(i, carry):
        to_twin(i).wait_recv()
        total = keep[i] + got[i]
        gate = total[:, 128:256]
        rounded[i, :, :128] = total[:, :128].astype(jnp.bfloat16)
        rounded[i, :, 128:] = (gate / (1.0 + jnp.exp(-gate))).astype(jnp.bfloat16)
        shared_sum[i] = total[:, 256:]

        @pl.when(i != mine)
        def _():
            xz_far(i).start()
            pl.when(has_bc)(bc_far(i).start)

        @pl.when(i == mine)
        def _():
            pltpu.make_async_copy(rounded.at[i], xz.at[mine], r_recv.at[mine]).start()

            @pl.when(has_bc)
            def _():
                pltpu.make_async_copy(
                    shared_sum.at[i], bc.at[bc_slot], c_recv.at[bc_slot]
                ).start()

        return carry

    lax.fori_loop(0, 8, hand_out, 0)

    for n, step in enumerate(TURNS):
        for h in range(2):
            came = (4 - step) % 4
            held = columns(0, came, h) if h == 0 else columns(came, 0, h)
            arrived(held, o1_recv.at[h, n])
            for m, onward in enumerate(TURNS):
                o_go(h, held, 2, 3 + n * 3 + m, onward, h == 0)

    step_copy.wait()
    step_sum = step_give[...] + step_got[...]
    step_raw = jnp.zeros((128, 16), jnp.float32)
    for t in range(4):
        step_raw += jnp.where(x_hi * 2 + core == t, step_sum[:, t * 16 : t * 16 + 16], 0.0)
    raw = step_raw + bias_ref[...]
    step_size = jnp.maximum(raw, 0.0) + jnp.log1p(jnp.exp(-jnp.abs(raw)))
    decay = jnp.exp(-jnp.exp(rate_ref[...]) * step_size)

    for slot in range(4):
        arrived(bc.at[slot], c_recv.at[slot])
    for copy in state_copies:
        copy.wait()

    def look(row, carry):
        steps_of = pl.ds(row, 4, stride=32)
        c_rows = jnp.concatenate([bc[2, steps_of, :], bc[3, steps_of, :]], axis=1)
        upper = c_rows.astype(jnp.bfloat16)
        lower = (c_rows - upper.astype(jnp.float32)).astype(jnp.bfloat16)
        seen = lax.dot_general(
            jnp.concatenate([upper, lower], axis=0),
            state[row],
            (((1,), (1,)), ((), ())),
            preferred_element_type=jnp.float32,
        )
        for t in range(4):
            read[pl.ds(t * 32 + row, 1), :] = seen[t : t + 1] + seen[t + 4 : t + 5]
        return carry

    lax.fori_loop(0, 32, look, 0, unroll=4)

    at = [slice(t * 32, t * 32 + 32) for t in range(4)]
    b = jnp.concatenate([bc[0], bc[1]], axis=1)
    c = jnp.concatenate([bc[2], bc[3]], axis=1)
    rows, total, coefs = [], None, []
    for t in range(4):
        total = decay[at[t]] if t == 0 else total * decay[at[t]]
        coefs = [member * decay[at[t]] for member in coefs] + [step_size[at[t]]]
        rows.append(total)
        for s in range(t + 1):
            term = coefs[s] * jnp.sum(b[at[s]] * c[at[t]], axis=1, keepdims=True)
            rows.append(term + skip_ref[...] if s == t else term)
    table = jnp.concatenate(rows, axis=0)
    head = lax.broadcasted_iota(jnp.int32, (16, 1024), 0)
    channel = lax.broadcasted_iota(jnp.int32, (16, 1024), 1)
    spread = jnp.where(channel // 64 == head, 1.0, 0.0).astype(jnp.float32)
    wide = jnp.dot(
        table, spread, precision=lax.Precision.HIGHEST, preferred_element_type=jnp.float32
    )

    for j in range(8):
        arrived(xz.at[j], r_recv.at[j])
    xs = [
        jnp.concatenate([xz[j, at[t], :128] for j in range(8)], axis=1).astype(jnp.float32)
        for t in range(4)
    ]
    k = 0
    for t in range(4):
        seen = wide[k * 32 : k * 32 + 32] * read[at[t], :]
        k += 1
        for s in range(t + 1):
            seen += wide[k * 32 : k * 32 + 32] * xs[s]
            k += 1
        gate = jnp.concatenate([xz[j, at[t], 128:] for j in range(8)], axis=1)
        gated = seen * gate.astype(jnp.float32)
        inv_rms = lax.rsqrt(jnp.mean(gated * gated, axis=1, keepdims=True) + eps)
        hid[x, at[t], :] = (gated * inv_rms * gain_ref[...]).astype(jnp.bfloat16)
        held = hid.at[x, pl.ds(t * 32, 32)]
        for n, step in enumerate(TURNS):
            copy = remote(
                held, held, h_send.at[n, t], h_recv.at[n, t], device(x + step, y, z, core)
            )
            copy.start()
            started.append(copy)

    for h in range(2):
        for n, came in enumerate((0, 3, 1, 2)):
            for m, step in enumerate(TURNS):
                away = (4 - step) % 4
                held = columns(away, came, h) if h == 0 else columns(came, away, h)
                arrived(held, o2_recv.at[h, n * 3 + m])
    for n, step in enumerate(TURNS):
        for t in range(4):
            arrived(hid.at[(x + 4 - step) % 4, pl.ds(t * 32, 32)], h_recv.at[n, t])

    def against(left, right):
        return lax.dot_general(
            left, right, (((1,), (1,)), ((), ())), preferred_element_type=jnp.float32
        )

    def partial(which):
        held = out_weights[which].reshape(512, 2048)
        return against(hid[0:2].reshape(256, 1024), held[:, :1024]) + against(
            hid[2:4].reshape(256, 1024), held[:, 1024:]
        )

    theirs = 1 - x_lo
    out_give[...] = partial(1 - core).reshape(2, 128, 512)

    def out_twin(i):
        return remote(out_give.at[i], out_got.at[i], e_send.at[i], e_recv.at[i], twin)

    out_twin(theirs).start()
    out_twin(x_lo).start()
    out_keep[...] = partial(core).reshape(2, 128, 512)
    half = pl.ds(pl.multiple_of(x_lo * 512, 512), 512)
    out_twin(theirs).wait_recv()
    back[...] = out_keep[theirs] + out_got[theirs]
    back_copy = remote(
        back,
        mix_ref.at[:, half],
        f_sem.at[0],
        f_sem.at[1],
        device(x_hi * 2 + theirs, y, z, core),
    )
    back_copy.start()
    out_twin(x_lo).wait_recv()
    mix_ref[:, half] = out_keep[x_lo] + out_got[x_lo]

    for copy in started:
        copy.wait_send()
    pl.when(jnp.logical_not(stays))(sent_on.wait_send)

    def sent(i, carry):
        to_twin(i).wait_send()

        @pl.when(i != mine)
        def _():
            xz_far(i).wait_send()
            pl.when(has_bc)(bc_far(i).wait_send)

        return carry

    lax.fori_loop(0, 8, sent, 0)
    out_twin(0).wait_send()
    out_twin(1).wait_send()
    back_copy.wait_send()
    arrived(mix_ref.at[:, pl.ds(pl.multiple_of(theirs * 512, 512), 512)], f_sem.at[1])


def mixer(pack, flat_in, out_weight, log_rate, step_bias, skip_gain, norm_gain, state):
    dma = pltpu.SemaphoreType.DMA
    vmem = pl.BlockSpec(memory_space=pltpu.VMEM)
    bf16, f32 = jnp.bfloat16, jnp.float32
    return pl.pallas_call(
        mixer_kernel,
        out_shape=jax.ShapeDtypeStruct((128, 1024), f32),
        in_specs=[vmem] * 7 + [pl.BlockSpec(memory_space=pl.ANY)],
        out_specs=vmem,
        scratch_shapes=[
            pltpu.VMEM((8, 128, 2048), bf16),
            pltpu.VMEM((4, 16, 176, 128), bf16),
            pltpu.VMEM((2048, 640), bf16),
            pltpu.VMEM((2048, 64), bf16),
            pltpu.VMEM((8, 128, 384), f32),
            pltpu.VMEM((8, 128, 384), f32),
            pltpu.VMEM((8, 128, 384), f32),
            pltpu.VMEM((8, 128, 256), bf16),
            pltpu.VMEM((8, 128, 128), f32),
            pltpu.VMEM((8, 128, 256), bf16),
            pltpu.VMEM((4, 128, 128), f32),
            pltpu.VMEM((128, 128), f32),
            pltpu.VMEM((128, 128), f32),
            pltpu.VMEM((32, 1024, 256), bf16),
            pltpu.VMEM((128, 1024), f32),
            pltpu.VMEM((2, 32, 2048), bf16),
            pltpu.VMEM((2, 4, 2, 2, 32, 2048), bf16),
            pltpu.VMEM((4, 128, 1024), bf16),
            pltpu.VMEM((2, 128, 512), f32),
            pltpu.VMEM((2, 128, 512), f32),
            pltpu.VMEM((2, 128, 512), f32),
            pltpu.VMEM((128, 512), f32),
            dma((4,)),
            dma((15,)),
            dma((2,)),
            dma((6,)),
            dma((6,)),
            dma((6,)),
            dma((6,)),
            dma((8,)),
            dma((8,)),
            dma((8,)),
            dma((8,)),
            dma((8,)),
            dma((8,)),
            dma((8,)),
            dma((4,)),
            dma((2,)),
            dma((3,)),
            dma((2,)),
            dma((2, 3)),
            dma((2, 3)),
            dma((2, 12)),
            dma((2, 12)),
            dma((3, 4)),
            dma((3, 4)),
            dma((2,)),
            dma((2,)),
            dma((2,)),
        ],
        compiler_params=pltpu.CompilerParams(
            collective_id=0, has_side_effects=True, vmem_limit_bytes=58 << 20
        ),
        cost_estimate=pl.CostEstimate(
            flops=4 << 30, bytes_accessed=200 << 20, transcendentals=0
        ),
        name="mixer",
    )(
        pack,
        flat_in,
        out_weight,
        log_rate.reshape(1, 16),
        step_bias.reshape(1, 16),
        skip_gain.reshape(1, 16),
        norm_gain.reshape(1, 1024),
        state,
    )


def shards(
    layer_in,
    lengths,
    prior_state,
    weight_x,
    weight_z,
    weight_b,
    weight_c,
    weight_step,
    weight_out,
    log_rate,
    step_bias,
    skip_gain,
    norm_gain,
):
    tensor = lax.axis_index("tensor")
    flat_in = layer_in.reshape(128, 4096)

    def by_chip(weight):
        return weight.reshape(32, 2, 2, 8, 128).transpose(1, 3, 2, 0, 4)

    def by_row(weight):
        return weight.reshape(32, 2, 4, 128).transpose(1, 2, 0, 3)

    pair = jnp.stack([by_chip(weight_x), by_chip(weight_z)], axis=3).reshape(16, 128, 128)
    shared = jnp.concatenate([by_row(weight_b), by_row(weight_c)], axis=1).reshape(16, 32, 128)
    fold = jnp.concatenate([weight_step[:16], weight_step[16:]], axis=1)
    fold = jnp.broadcast_to(fold[None], (16, 16, 128))
    pack = jnp.concatenate([pair, shared, fold], axis=1)
    out_weight = (
        weight_out.T.reshape(32, 2, 2, 1024).transpose(2, 0, 1, 3).reshape(2, 32, 2048)
    )
    mix = mixer(
        pack,
        flat_in,
        out_weight,
        log_rate,
        step_bias,
        skip_gain,
        norm_gain,
        prior_state.reshape(32, 1024, 256),
    ).reshape(4, 32, 1024)
    residual = lax.dynamic_slice_in_dim(layer_in, tensor * 1024, 1024, 2).astype(jnp.float32)
    active = lengths[None, :] > jnp.arange(4, dtype=jnp.int32)[:, None]
    return jnp.where(active[:, :, None], residual + mix, residual).astype(jnp.bfloat16)


def solution(mesh):
    placed = (
        P(None, "group", None),
        P("group"),
        P("group", "tensor", None, None),
        P(("group", "tensor"), None),
        P(("group", "tensor"), None),
        P(("group", "tensor"), None),
        P(("group", "tensor"), None),
        P(("group", "tensor"), None),
        P(None, ("group", "tensor")),
        P("tensor"),
        P("tensor"),
        P("tensor"),
        P("tensor"),
    )
    return jax.shard_map(
        shards, mesh=mesh, in_specs=placed, out_specs=P(None, "group", "tensor"), check_vma=False
    )
```

```python
import jax
import jax.numpy as jnp
from jax import lax
from jax.experimental import pallas as pl
from jax.experimental.pallas import tpu as pltpu
from jax.sharding import PartitionSpec as P

MESH = pl.DeviceIdType.MESH
eps = 1e-05


def here():
    group, tensor = lax.axis_index("group"), lax.axis_index("tensor")
    return (tensor // 2) * 2 + group // 16, (group // 4) % 4, group % 4, tensor % 2


def device(x, y, z, core):
    return ((x % 2) * 16 + (y % 4) * 4 + z % 4, ((x % 4) // 2) * 2 + core % 2)


def remote(source, target, send_sem, recv_sem, where):
    return pltpu.make_async_remote_copy(
        src_ref=source,
        dst_ref=target,
        send_sem=send_sem,
        recv_sem=recv_sem,
        device_id=where,
        device_id_type=MESH,
    )


def arrived(ref, sem):
    pltpu.make_async_copy(ref, ref, sem).wait()


TURNS = (1, 3, 2)


def mixer_kernel(
    x_ref,
    z_ref,
    b_ref,
    c_ref,
    fold_ref,
    act_ref,
    out_weight_ref,
    rate_ref,
    bias_ref,
    skip_ref,
    gain_ref,
    state_ref,
    mix_ref,
    pack,
    act,
    landed,
    weights,
    step_weights,
    keep,
    give,
    got,
    rounded,
    shared,
    shared_got,
    xz,
    bc,
    step_give,
    step_got,
    state,
    read,
    quarter,
    out_weights,
    hid,
    out_keep,
    out_give,
    out_got,
    back,
    s_sem,
    g_send,
    g_recv,
    a_send,
    a_recv,
    b_send,
    b_recv,
    z_send,
    z_recv,
    x_send,
    x_recv,
    d_send,
    d_recv,
    r_send,
    r_recv,
    c_send,
    c_recv,
    t_sem,
    q_sem,
    w_sem,
    o_send,
    o_recv,
    h_send,
    h_recv,
    e_send,
    e_recv,
    f_send,
    f_recv,
):
    x, y, z, core = here()
    x_lo, x_hi = x % 2, x // 2
    mine = x_lo * 4 + z
    twin = device(x, y, z, core + 1)
    started = []

    target_x, target_y = x_lo * 2 + y % 2, y + x_hi
    stays = jnp.logical_and(target_x == x, x_hi == 0)
    k_here = (y - x_lo + 4) % 4
    source = device((k_here % 2) * 2 + x_hi, (k_here // 2) * 2 + x_lo, z, core)

    barrier = pltpu.get_barrier_semaphore()

    def signal(where):
        pl.semaphore_signal(barrier, inc=1, device_id=where, device_id_type=MESH)

    plane = [(dx, dz) for dz in (2, 1, 3, 0) for dx in (2, 1, 3, 0)]
    for dx, dz in plane[:-1]:
        signal(device(x + dx, y, z + dz, core))
    for step in TURNS:
        signal(device(x, y + step, z, core))
    signal(twin)
    pl.when(jnp.logical_not(stays))(lambda: signal(source))

    lane = lax.broadcasted_iota(jnp.int32, (256, 128), 1)
    from_lane = lax.broadcasted_iota(jnp.int32, (256, 128), 0)
    chosen = from_lane == (lane // 32) * 64 + core * 32 + lane % 32
    picker = jnp.where(chosen, 1.0, 0.0).astype(jnp.bfloat16)
    for i in range(16):
        spot = ((i % 8) // 2) * 4 + (i // 8) * 2 + i % 2
        act[mine, :, spot * 128 : spot * 128 + 128] = jnp.dot(
            act_ref[:, i * 256 : i * 256 + 256], picker, preferred_element_type=jnp.float32
        ).astype(jnp.bfloat16)

    fold = jnp.concatenate([fold_ref[:16], fold_ref[16:]], axis=1)
    for hi in range(2):
        for j in range(8):
            to = hi * 8 + j
            for half in range(2):
                lanes = slice((hi * 16 + half * 8 + j) * 128, (hi * 16 + half * 8 + j + 1) * 128)
                pack[to, half * 64 : half * 64 + 32] = x_ref[:, lanes]
                pack[to, half * 64 + 32 : half * 64 + 64] = z_ref[:, lanes]
            lanes = slice((hi * 4 + j % 4) * 128, (hi * 4 + j % 4 + 1) * 128)
            pack[to, 128:160] = (b_ref if j < 4 else c_ref)[:, lanes]
            pack[to, 160:176] = fold
    for hi in range(2):
        quarter[core, :, hi * 1024 : hi * 1024 + 1024] = out_weight_ref[
            :, pl.ds(pl.multiple_of((hi * 2 + core) * 1024, 1024), 1024)
        ]

    pl.semaphore_wait(barrier, 20 - jnp.where(stays, 1, 0))

    parts = (pl.ds(0, 96), pl.ds(96, 80))
    landing = landed.at[y, x_lo * 8 + z * 2 + x_hi]
    for p in range(2):
        for n, (dx, dz) in enumerate(plane):
            xd, zd = (x + dx) % 4, (z + dz) % 4
            tile = pack.at[(xd // 2) * 8 + (xd % 2) * 4 + zd, parts[p]]
            to = landing.at[parts[p]]
            if n == 15:
                pltpu.make_async_copy(tile, to, a_recv.at[p]).start()
            else:
                copy = remote(tile, to, a_send.at[p, n], a_recv.at[p], device(xd, y, zd, core))
                copy.start()
                started.append(copy)

    def piece(dz, h):
        return act.at[x_lo * 4 + (z + dz) % 4, pl.ds(h * 64, 64)]

    def other(dz, h):
        return act.at[(1 - x_lo) * 4 + (z + dz) % 4, pl.ds(h * 64, 64)]

    def z_go(dz, h, slot, step, ref=piece):
        copy = remote(
            ref(dz, h),
            ref(dz, h),
            z_send.at[slot],
            z_recv.at[slot],
            device(x, y, z + step, core),
        )
        copy.start()
        started.append(copy)

    def x_go(dz, h, rel):
        slot = rel * 2 + h
        copy = remote(
            piece(dz, h),
            piece(dz, h),
            x_send.at[slot],
            x_recv.at[slot],
            device(x + (1 if h == 0 else 3), y, z, core),
        )
        copy.start()
        started.append(copy)

    z_go(0, 0, 0, 1)
    z_go(0, 1, 3, 3)
    x_go(0, 0, 0)
    x_go(0, 1, 0)
    z_go(0, 1, 1, 1)
    z_go(0, 0, 2, 3)

    for hi in range(2):
        copy = remote(
            out_weight_ref.at[:, pl.ds(pl.multiple_of((hi * 2 + 1 - core) * 1024, 1024), 1024)],
            quarter.at[core, :, pl.ds(hi * 1024, 1024)],
            q_sem.at[hi],
            q_sem.at[2 + hi],
            twin,
        )
        copy.start()
        started.append(copy)

    state_copies = [
        pltpu.make_async_copy(
            state_ref.at[pl.ds(n * 8, 8)], state.at[pl.ds(n * 8, 8)], s_sem.at[n]
        )
        for n in range(4)
    ]
    for copy in state_copies:
        copy.start()

    def block(dy, h, p):
        return landed.at[(y + dy) % 4, pl.ds(h * 8, 8), parts[p]]

    def y_go(dy, h, p, slot, step):
        copy = remote(
            block(dy, h, p),
            block(dy, h, p),
            b_send.at[p, slot],
            b_recv.at[p, slot],
            device(x, y + step, z, core),
        )
        copy.start()
        started.append(copy)

    def y_forward(p):
        arrived(block(3, 0, p), b_recv.at[p, 0])
        y_go(3, 0, p, 4, 1)
        arrived(block(1, 1, p), b_recv.at[p, 3])
        y_go(1, 1, p, 5, 3)

    def lay_out(dy):
        at = (y + dy) % 4
        rows = pl.ds(pl.multiple_of(at * 512, 512), 512)
        for n in range(5):
            weights[rows, n * 128 : n * 128 + 128] = landed[
                at, :, n * 32 : n * 32 + 32, :
            ].reshape(512, 128)
        pairs = landed[at, :, 160:176, :]
        step_weights[rows, :] = jnp.concatenate(
            [pairs[:, :, :64], pairs[:, :, 64:]], axis=1
        ).reshape(512, 64)

    for p in range(2):
        arrived(landed.at[y, :, parts[p]], a_recv.at[p])
        y_go(0, 0, p, 0, 1)
        y_go(0, 1, p, 3, 3)
        y_go(0, 1, p, 1, 1)
        y_go(0, 0, p, 2, 3)

    arrived(piece(3, 0), z_recv.at[0])
    z_go(3, 0, 4, 1)
    x_go(3, 0, 1)
    arrived(piece(1, 1), z_recv.at[3])
    z_go(1, 1, 5, 3)
    x_go(1, 1, 2)
    y_forward(0)
    arrived(piece(3, 1), z_recv.at[1])
    x_go(3, 1, 1)
    arrived(piece(1, 0), z_recv.at[2])
    x_go(1, 0, 2)
    for hi in range(2):
        arrived(quarter.at[1 - core, :, pl.ds(hi * 1024, 1024)], q_sem.at[2 + hi])
    sent_on = remote(
        quarter,
        out_weights.at[y // 2, z, x_hi],
        w_sem.at[0],
        w_sem.at[1],
        device(target_x, target_y, z, core),
    )
    kept = pltpu.make_async_copy(quarter, out_weights.at[y // 2, z, x_hi], w_sem.at[1])
    pl.when(jnp.logical_not(stays))(sent_on.start)
    pl.when(stays)(kept.start)
    lay_out(0)
    arrived(other(3, 0), x_recv.at[2])
    z_go(3, 0, 6, 1, other)
    arrived(other(1, 1), x_recv.at[5])
    z_go(1, 1, 7, 3, other)
    y_forward(1)

    arrived(block(3, 1, 0), b_recv.at[0, 1])
    arrived(block(3, 1, 1), b_recv.at[1, 1])
    lay_out(3)
    arrived(block(1, 0, 0), b_recv.at[0, 2])
    arrived(block(1, 0, 1), b_recv.at[1, 2])
    lay_out(1)
    arrived(piece(2, 0), z_recv.at[4])
    arrived(piece(2, 1), z_recv.at[5])
    arrived(other(0, 0), x_recv.at[0])
    arrived(other(0, 1), x_recv.at[1])
    arrived(other(3, 1), x_recv.at[3])
    arrived(other(1, 0), x_recv.at[4])

    def columns(dk, dz, h):
        k = (k_here + dk) % 4
        return out_weights.at[k // 2, (z + dz) % 4, k % 2, h]

    def along(h, stage):
        return (h == 1) == (stage == 1)

    def unit(h, stage, unit_at, away):
        if along(h, stage):
            return columns(away, unit_at, h)
        return columns(unit_at, away, h)

    def o_go(h, stage, unit_at, away, slot, step, part=None):
        held = unit(h, stage, unit_at, away)
        if part is not None:
            held = held.at[pl.ds(part * 16, 16)]
        where = device(x, y + step, z, core) if along(h, stage) else device(x, y, z + step, core)
        index = (stage - 1) * 8 + unit_at * (stage - 1) * 4 + h * (4 if stage == 1 else 16) + slot
        copy = remote(held, held, o_send.at[index], o_recv.at[index], where)
        copy.start()
        started.append(copy)

    def o_wait(h, stage, unit_at, away, slot, part=None):
        held = unit(h, stage, unit_at, away)
        if part is not None:
            held = held.at[pl.ds(part * 16, 16)]
        index = (stage - 1) * 8 + unit_at * (stage - 1) * 4 + h * (4 if stage == 1 else 16) + slot
        arrived(held, o_recv.at[index])

    def o_both(h, stage, unit_at):
        o_go(h, stage, unit_at, 0, 0, 1)
        o_go(h, stage, unit_at, 0, 1, 3)

    def o_forward(h, stage, unit_at):
        o_wait(h, stage, unit_at, 3, 0)
        o_go(h, stage, unit_at, 3, 2, 1, 0)
        o_wait(h, stage, unit_at, 1, 1)
        o_go(h, stage, unit_at, 1, 3, 3, 1)

    def o_last(h, stage, unit_at):
        o_wait(h, stage, unit_at, 2, 2, 0)
        o_wait(h, stage, unit_at, 2, 3, 1)

    def o_begin():
        arrived(out_weights.at[k_here // 2, z, k_here % 2], w_sem.at[1])
        for h in range(2):
            o_both(h, 1, 0)
        for h in range(2):
            o_both(h, 2, 0)

    def o_second():
        for h in range(2):
            o_forward(h, 1, 0)
            o_both(h, 2, 3)
            o_both(h, 2, 1)

    def o_third():
        for h in range(2):
            o_last(h, 1, 0)
            o_both(h, 2, 2)
        for h in range(2):
            o_forward(h, 2, 0)

    def o_fourth():
        for h in range(2):
            o_forward(h, 2, 3)
            o_forward(h, 2, 1)

    def o_fifth():
        for h in range(2):
            o_forward(h, 2, 2)

    def o_end():
        for h in range(2):
            for unit_at in range(4):
                o_last(h, 2, unit_at)

    o_begin()
    for p in range(2):
        arrived(block(2, 0, p), b_recv.at[p, 4])
        arrived(block(2, 1, p), b_recv.at[p, 5])
    lay_out(2)
    arrived(other(2, 0), z_recv.at[6])
    arrived(other(2, 1), z_recv.at[7])

    def to_twin(i):
        return remote(give.at[i], got.at[i], d_send.at[i], d_recv.at[i], twin)

    step_half = jnp.dot(act[mine], step_weights[...], preferred_element_type=jnp.float32)
    step_give[...] = jnp.concatenate([step_half, step_half], axis=1)
    step_copy = remote(step_give, step_got, t_sem.at[0], t_sem.at[1], twin)
    step_copy.start()

    bc_slot = x_lo * 2 + z % 2
    has_bc = core == z // 2

    def bc_twin(i):
        two = pl.ds(i * 2, 2)
        return remote(shared.at[two], shared_got.at[two], g_send.at[i], g_recv.at[i], twin)

    def multiply_bc(i, carry):
        two = pl.ds(i * 2, 2)
        shared[two] = jnp.dot(
            act[two].reshape(256, 2048), weights[:, 512:], preferred_element_type=jnp.float32
        ).reshape(2, 128, 128)
        pl.when(jnp.logical_not(has_bc))(bc_twin(i).start)
        return carry

    lax.fori_loop(0, 4, multiply_bc, 0)

    def multiply(i, carry):
        product = jnp.dot(act[i], weights[:, :512], preferred_element_type=jnp.float32)
        first, second = product[:, :256], product[:, 256:]
        keep[i] = jnp.where(core == 0, first, second)
        give[i] = jnp.where(core == 0, second, first)
        to_twin(i).start()
        return carry

    def owner(i):
        return device(x_hi * 2 + i // 4, y, i % 4, core)

    def xz_far(i):
        return remote(rounded.at[i], xz.at[mine], r_send.at[i], r_recv.at[mine], owner(i))

    def bc_far(i):
        return remote(shared.at[i], bc.at[bc_slot], c_send.at[i], c_recv.at[bc_slot], owner(i))

    lax.fori_loop(0, 4, multiply, 0)

    @pl.when(has_bc)
    def _():
        for i in range(4):
            two = pl.ds(i * 2, 2)
            bc_twin(i).wait_recv()
            shared[two] = shared[two] + shared_got[two]

        def hand_out_bc(i, carry):
            pl.when(i != mine)(lambda: bc_far(i).start())

            @pl.when(i == mine)
            def _():
                pltpu.make_async_copy(
                    shared.at[i], bc.at[bc_slot], c_recv.at[bc_slot]
                ).start()

            return carry

        lax.fori_loop(0, 8, hand_out_bc, 0)

    o_second()
    lax.fori_loop(4, 8, multiply, 0)

    def hand_out(i, carry):
        to_twin(i).wait_recv()
        total = keep[i] + got[i]
        gate = total[:, 128:]
        rounded[i, :, :128] = total[:, :128].astype(jnp.bfloat16)
        rounded[i, :, 128:] = (gate / (1.0 + jnp.exp(-gate))).astype(jnp.bfloat16)
        pl.when(i != mine)(lambda: xz_far(i).start())

        @pl.when(i == mine)
        def _():
            pltpu.make_async_copy(rounded.at[i], xz.at[mine], r_recv.at[mine]).start()

        return carry

    lax.fori_loop(0, 8, hand_out, 0)
    o_third()

    step_copy.wait()
    step_sum = step_give[...] + step_got[...]
    step_raw = jnp.zeros((128, 16), jnp.float32)
    for t in range(4):
        step_raw += jnp.where(x_hi * 2 + core == t, step_sum[:, t * 16 : t * 16 + 16], 0.0)
    raw = step_raw + bias_ref[...]
    step_size = jnp.maximum(raw, 0.0) + jnp.log1p(jnp.exp(-jnp.abs(raw)))
    decay = jnp.exp(-jnp.exp(rate_ref[...]) * step_size)

    for slot in range(4):
        arrived(bc.at[slot], c_recv.at[slot])
    for copy in state_copies:
        copy.wait()

    def look(row, carry):
        steps_of = pl.ds(row, 4, stride=32)
        c_rows = jnp.concatenate([bc[2, steps_of, :], bc[3, steps_of, :]], axis=1)
        upper = c_rows.astype(jnp.bfloat16)
        lower = (c_rows - upper.astype(jnp.float32)).astype(jnp.bfloat16)
        seen = lax.dot_general(
            jnp.concatenate([upper, lower], axis=0),
            state[row],
            (((1,), (1,)), ((), ())),
            preferred_element_type=jnp.float32,
        )
        for t in range(4):
            read[pl.ds(t * 32 + row, 1), :] = seen[t : t + 1] + seen[t + 4 : t + 5]
        return carry

    lax.fori_loop(0, 16, look, 0, unroll=4)
    o_fourth()
    lax.fori_loop(16, 32, look, 0, unroll=4)

    at = [slice(t * 32, t * 32 + 32) for t in range(4)]
    b = jnp.concatenate([bc[0], bc[1]], axis=1)
    c = jnp.concatenate([bc[2], bc[3]], axis=1)
    rows, total, coefs = [], None, []
    for t in range(4):
        total = decay[at[t]] if t == 0 else total * decay[at[t]]
        coefs = [member * decay[at[t]] for member in coefs] + [step_size[at[t]]]
        rows.append(total)
        for s in range(t + 1):
            term = coefs[s] * jnp.sum(b[at[s]] * c[at[t]], axis=1, keepdims=True)
            rows.append(term + skip_ref[...] if s == t else term)
    table = jnp.concatenate(rows, axis=0)
    head = lax.broadcasted_iota(jnp.int32, (16, 1024), 0)
    channel = lax.broadcasted_iota(jnp.int32, (16, 1024), 1)
    spread = jnp.where(channel // 64 == head, 1.0, 0.0).astype(jnp.float32)
    wide = jnp.dot(
        table, spread, precision=lax.Precision.HIGHEST, preferred_element_type=jnp.float32
    )

    o_fifth()
    for j in range(8):
        arrived(xz.at[j], r_recv.at[j])

    def hid_part(block, away, part=None):
        rows_of = pl.ds(block * 64, 64) if part is None else pl.ds(block * 64 + part * 32, 32)
        return hid.at[(x + away) % 4, rows_of]

    def h_go(block, away, slot, step, part=None):
        held = hid_part(block, away, part)
        copy = remote(
            held, held, h_send.at[block, slot], h_recv.at[block, slot], device(x + step, y, z, core)
        )
        copy.start()
        started.append(copy)

    def h_forward(block):
        arrived(hid_part(block, 3), h_recv.at[block, 0])
        h_go(block, 3, 2, 1, 0)
        arrived(hid_part(block, 1), h_recv.at[block, 1])
        h_go(block, 1, 3, 3, 1)

    def h_last(block):
        arrived(hid_part(block, 2, 0), h_recv.at[block, 2])
        arrived(hid_part(block, 2, 1), h_recv.at[block, 3])

    for block in range(2):
        sixteen = [slice(t * 32 + block * 16, t * 32 + block * 16 + 16) for t in range(4)]
        xs = [
            jnp.concatenate([xz[j, sixteen[t], :128] for j in range(8)], axis=1).astype(
                jnp.float32
            )
            for t in range(4)
        ]
        k = block * 16
        for t in range(4):
            seen = wide[k : k + 16] * read[sixteen[t], :]
            k += 32
            for s in range(t + 1):
                seen += wide[k : k + 16] * xs[s]
                k += 32
            gate = jnp.concatenate([xz[j, sixteen[t], 128:] for j in range(8)], axis=1)
            gated = seen * gate.astype(jnp.float32)
            inv_rms = lax.rsqrt(jnp.mean(gated * gated, axis=1, keepdims=True) + eps)
            hid[x, block * 64 + t * 16 : block * 64 + t * 16 + 16, :] = (
                gated * inv_rms * gain_ref[...]
            ).astype(jnp.bfloat16)
        h_go(block, 0, 0, 1)
        h_go(block, 0, 1, 3)

    h_forward(0)
    h_last(0)
    h_forward(1)
    o_end()

    def against(left, right):
        return lax.dot_general(
            left, right, (((1,), (1,)), ((), ())), preferred_element_type=jnp.float32
        )

    def partial(block, which):
        held = out_weights[which].reshape(512, 2048)
        rows_of = slice(block * 64, block * 64 + 64)
        product = against(hid[0:2, rows_of].reshape(128, 1024), held[:, :1024]) + against(
            hid[2:4, rows_of].reshape(128, 1024), held[:, 1024:]
        )
        return product.reshape(2, 64, 512)

    theirs = 1 - x_lo
    half = pl.ds(pl.multiple_of(x_lo * 512, 512), 512)

    def out_twin(block):
        return remote(
            out_give.at[block], out_got.at[block], e_send.at[block], e_recv.at[block], twin
        )

    def back_copy(block):
        return remote(
            back.at[block],
            mix_ref.at[:, pl.ds(block * 16, 16), half],
            f_send.at[block],
            f_recv.at[block],
            device(x_hi * 2 + theirs, y, z, core),
        )

    def give_out(block):
        out_give[block] = partial(block, 1 - core)
        out_twin(block).start()

    def join(block):
        out_twin(block).wait_recv()
        back[block] = (out_keep[block, theirs] + out_got[block, theirs]).reshape(4, 16, 512)
        back_copy(block).start()
        mix_ref[:, block * 16 : block * 16 + 16, half] = (
            out_keep[block, x_lo] + out_got[block, x_lo]
        ).reshape(4, 16, 512)

    give_out(0)
    out_keep[0] = partial(0, core)
    h_last(1)
    give_out(1)
    join(0)
    out_keep[1] = partial(1, core)
    join(1)

    for copy in started:
        copy.wait_send()
    pl.when(jnp.logical_not(stays))(sent_on.wait_send)

    def sent(i, carry):
        to_twin(i).wait_send()

        @pl.when(i != mine)
        def _():
            xz_far(i).wait_send()
            pl.when(has_bc)(bc_far(i).wait_send)

        return carry

    lax.fori_loop(0, 8, sent, 0)

    @pl.when(jnp.logical_not(has_bc))
    def _():
        for i in range(4):
            bc_twin(i).wait_send()

    for block in range(2):
        out_twin(block).wait_send()
        back_copy(block).wait_send()
        arrived(
            mix_ref.at[:, pl.ds(block * 16, 16), pl.ds(pl.multiple_of(theirs * 512, 512), 512)],
            f_recv.at[block],
        )


def mixer(weight_x, weight_z, weight_b, weight_c, weight_step, flat_in, out_weight, log_rate, step_bias, skip_gain, norm_gain, state):
    dma = pltpu.SemaphoreType.DMA
    vmem = pl.BlockSpec(memory_space=pltpu.VMEM)
    bf16, f32 = jnp.bfloat16, jnp.float32
    return pl.pallas_call(
        mixer_kernel,
        out_shape=jax.ShapeDtypeStruct((4, 32, 1024), f32),
        in_specs=[vmem] * 11 + [pl.BlockSpec(memory_space=pl.ANY)],
        out_specs=vmem,
        scratch_shapes=[
            pltpu.VMEM((16, 176, 128), bf16),
            pltpu.VMEM((8, 128, 2048), bf16),
            pltpu.VMEM((4, 16, 176, 128), bf16),
            pltpu.VMEM((2048, 640), bf16),
            pltpu.VMEM((2048, 64), bf16),
            pltpu.VMEM((8, 128, 256), f32),
            pltpu.VMEM((8, 128, 256), f32),
            pltpu.VMEM((8, 128, 256), f32),
            pltpu.VMEM((8, 128, 256), bf16),
            pltpu.VMEM((8, 128, 128), f32),
            pltpu.VMEM((8, 128, 128), f32),
            pltpu.VMEM((8, 128, 256), bf16),
            pltpu.VMEM((4, 128, 128), f32),
            pltpu.VMEM((128, 128), f32),
            pltpu.VMEM((128, 128), f32),
            pltpu.VMEM((32, 1024, 256), bf16),
            pltpu.VMEM((128, 1024), f32),
            pltpu.VMEM((2, 32, 2048), bf16),
            pltpu.VMEM((2, 4, 2, 2, 32, 2048), bf16),
            pltpu.VMEM((4, 128, 1024), bf16),
            pltpu.VMEM((2, 2, 64, 512), f32),
            pltpu.VMEM((2, 2, 64, 512), f32),
            pltpu.VMEM((2, 2, 64, 512), f32),
            pltpu.VMEM((2, 4, 16, 512), f32),
            dma((4,)),
            dma((4,)),
            dma((4,)),
            dma((2, 15)),
            dma((2,)),
            dma((2, 6)),
            dma((2, 6)),
            dma((8,)),
            dma((8,)),
            dma((6,)),
            dma((6,)),
            dma((8,)),
            dma((8,)),
            dma((8,)),
            dma((8,)),
            dma((8,)),
            dma((4,)),
            dma((2,)),
            dma((4,)),
            dma((2,)),
            dma((40,)),
            dma((40,)),
            dma((2, 4)),
            dma((2, 4)),
            dma((2,)),
            dma((2,)),
            dma((2,)),
            dma((2,)),
        ],
        compiler_params=pltpu.CompilerParams(
            collective_id=0, has_side_effects=True, vmem_limit_bytes=58 << 20
        ),
        cost_estimate=pl.CostEstimate(
            flops=4 << 30, bytes_accessed=200 << 20, transcendentals=0
        ),
        name="mixer",
    )(
        weight_x,
        weight_z,
        weight_b,
        weight_c,
        weight_step,
        flat_in,
        out_weight,
        log_rate.reshape(1, 16),
        step_bias.reshape(1, 16),
        skip_gain.reshape(1, 16),
        norm_gain.reshape(1, 1024),
        state,
    )


def shards(
    layer_in,
    lengths,
    prior_state,
    weight_x,
    weight_z,
    weight_b,
    weight_c,
    weight_step,
    weight_out,
    log_rate,
    step_bias,
    skip_gain,
    norm_gain,
):
    tensor = lax.axis_index("tensor")
    flat_in = layer_in.reshape(128, 4096)

    mix = mixer(
        weight_x,
        weight_z,
        weight_b,
        weight_c,
        weight_step,
        flat_in,
        weight_out.T,
        log_rate,
        step_bias,
        skip_gain,
        norm_gain,
        prior_state.reshape(32, 1024, 256),
    )
    residual = lax.dynamic_slice_in_dim(layer_in, tensor * 1024, 1024, 2).astype(jnp.float32)
    active = lengths[None, :] > jnp.arange(4, dtype=jnp.int32)[:, None]
    return jnp.where(active[:, :, None], residual + mix, residual).astype(jnp.bfloat16)


def solution(mesh):
    placed = (
        P(None, "group", None),
        P("group"),
        P("group", "tensor", None, None),
        P(("group", "tensor"), None),
        P(("group", "tensor"), None),
        P(("group", "tensor"), None),
        P(("group", "tensor"), None),
        P(("group", "tensor"), None),
        P(None, ("group", "tensor")),
        P("tensor"),
        P("tensor"),
        P("tensor"),
        P("tensor"),
    )
    return jax.shard_map(
        shards, mesh=mesh, in_specs=placed, out_specs=P(None, "group", "tensor"), check_vma=False
    )
```

```python
import jax
import jax.numpy as jnp
from jax import lax
from jax.experimental import pallas as pl
from jax.experimental.pallas import tpu as pltpu
from jax.sharding import PartitionSpec as P

MESH = pl.DeviceIdType.MESH
eps = 1e-05


def here():
    group, tensor = lax.axis_index("group"), lax.axis_index("tensor")
    return (tensor // 2) * 2 + group // 16, (group // 4) % 4, group % 4, tensor % 2


def device(x, y, z, core):
    return ((x % 2) * 16 + (y % 4) * 4 + z % 4, ((x % 4) // 2) * 2 + core % 2)


def remote(source, target, send_sem, recv_sem, where):
    return pltpu.make_async_remote_copy(
        src_ref=source,
        dst_ref=target,
        send_sem=send_sem,
        recv_sem=recv_sem,
        device_id=where,
        device_id_type=MESH,
    )


def arrived(ref, sem):
    pltpu.make_async_copy(ref, ref, sem).wait()


TURNS = (1, 3, 2)


def mixer_kernel(
    x_ref,
    z_ref,
    b_ref,
    c_ref,
    fold_ref,
    act_ref,
    out_weight_ref,
    rate_ref,
    bias_ref,
    skip_ref,
    gain_ref,
    length_ref,
    state_ref,
    out_ref,
    pack,
    act,
    landed,
    weights,
    step_weights,
    keep,
    give,
    got,
    rounded,
    shared,
    shared_got,
    xz,
    bc,
    step_give,
    step_got,
    state,
    read,
    quarter,
    out_weights,
    hid,
    out_keep,
    out_give,
    out_got,
    back,
    ours,
    theirs_in,
    s_sem,
    g_send,
    g_recv,
    a_send,
    a_recv,
    b_send,
    b_recv,
    z_send,
    z_recv,
    x_send,
    x_recv,
    d_send,
    d_recv,
    r_send,
    r_recv,
    c_send,
    c_recv,
    t_sem,
    q_sem,
    w_sem,
    o_send,
    o_recv,
    h_send,
    h_recv,
    e_send,
    e_recv,
    f_send,
    f_recv,
):
    x, y, z, core = here()
    x_lo, x_hi = x % 2, x // 2
    mine = x_lo * 4 + z
    twin = device(x, y, z, core + 1)
    started = []

    target_x = x_lo * 2 + x_hi
    stays = target_x == x

    barrier = pltpu.get_barrier_semaphore()

    def signal(where):
        pl.semaphore_signal(barrier, inc=1, device_id=where, device_id_type=MESH)

    plane = [(dx, dz) for dz in (2, 1, 3, 0) for dx in (2, 1, 3, 0)]
    for dx, dz in plane[:-1]:
        signal(device(x + dx, y, z + dz, core))
    for step in TURNS:
        signal(device(x, y + step, z, core))
    signal(twin)
    pl.when(jnp.logical_not(stays))(lambda: signal(device(target_x, y, z, core)))

    lane = lax.broadcasted_iota(jnp.int32, (256, 128), 1)
    from_lane = lax.broadcasted_iota(jnp.int32, (256, 128), 0)
    chosen = from_lane == (lane // 32) * 64 + core * 32 + lane % 32
    picker = jnp.where(chosen, 1.0, 0.0).astype(jnp.bfloat16)
    for i in range(16):
        spot = ((i % 8) // 2) * 4 + (i // 8) * 2 + i % 2
        act[mine, :, spot * 128 : spot * 128 + 128] = jnp.dot(
            act_ref[:, i * 256 : i * 256 + 256], picker, preferred_element_type=jnp.float32
        ).astype(jnp.bfloat16)

    fold = jnp.concatenate([fold_ref[:16], fold_ref[16:]], axis=1)
    for hi in range(2):
        for j in range(8):
            to = hi * 8 + j
            for half in range(2):
                lanes = slice((hi * 16 + half * 8 + j) * 128, (hi * 16 + half * 8 + j + 1) * 128)
                pack[to, half * 64 : half * 64 + 32] = x_ref[:, lanes]
                pack[to, half * 64 + 32 : half * 64 + 64] = z_ref[:, lanes]
            lanes = slice((hi * 4 + j % 4) * 128, (hi * 4 + j % 4 + 1) * 128)
            pack[to, 128:160] = (b_ref if j < 4 else c_ref)[:, lanes]
            pack[to, 160:176] = fold
    for hi in range(2):
        quarter[core, :, hi * 1024 : hi * 1024 + 1024] = out_weight_ref[
            :, pl.ds(pl.multiple_of((hi * 2 + core) * 1024, 1024), 1024)
        ]

    pl.semaphore_wait(barrier, 20 - jnp.where(stays, 1, 0))

    parts = (pl.ds(0, 96), pl.ds(96, 80))
    landing = landed.at[y, x_lo * 8 + z * 2 + x_hi]
    for p in range(2):
        for n, (dx, dz) in enumerate(plane):
            xd, zd = (x + dx) % 4, (z + dz) % 4
            tile = pack.at[(xd // 2) * 8 + (xd % 2) * 4 + zd, parts[p]]
            to = landing.at[parts[p]]
            if n == 15:
                pltpu.make_async_copy(tile, to, a_recv.at[p]).start()
            else:
                copy = remote(tile, to, a_send.at[p, n], a_recv.at[p], device(xd, y, zd, core))
                copy.start()
                started.append(copy)

    def piece(dz, h):
        return act.at[x_lo * 4 + (z + dz) % 4, pl.ds(h * 64, 64)]

    def other(dz, h):
        return act.at[(1 - x_lo) * 4 + (z + dz) % 4, pl.ds(h * 64, 64)]

    def z_go(dz, h, slot, step, ref=piece):
        copy = remote(
            ref(dz, h),
            ref(dz, h),
            z_send.at[slot],
            z_recv.at[slot],
            device(x, y, z + step, core),
        )
        copy.start()
        started.append(copy)

    def x_go(dz, h, rel):
        slot = rel * 2 + h
        copy = remote(
            piece(dz, h),
            piece(dz, h),
            x_send.at[slot],
            x_recv.at[slot],
            device(x + (1 if h == 0 else 3), y, z, core),
        )
        copy.start()
        started.append(copy)

    z_go(0, 0, 0, 1)
    z_go(0, 1, 3, 3)
    x_go(0, 0, 0)
    x_go(0, 1, 0)
    z_go(0, 1, 1, 1)
    z_go(0, 0, 2, 3)

    for hi in range(2):
        copy = remote(
            out_weight_ref.at[:, pl.ds(pl.multiple_of((hi * 2 + 1 - core) * 1024, 1024), 1024)],
            quarter.at[core, :, pl.ds(hi * 1024, 1024)],
            q_sem.at[hi],
            q_sem.at[2 + hi],
            twin,
        )
        copy.start()
        started.append(copy)

    state_copies = [
        pltpu.make_async_copy(
            state_ref.at[pl.ds(n * 8, 8)], state.at[pl.ds(n * 8, 8)], s_sem.at[n]
        )
        for n in range(4)
    ]
    for copy in state_copies:
        copy.start()

    def block(dy, h, p):
        return landed.at[(y + dy) % 4, pl.ds(h * 8, 8), parts[p]]

    def y_go(dy, h, p, slot, step):
        copy = remote(
            block(dy, h, p),
            block(dy, h, p),
            b_send.at[p, slot],
            b_recv.at[p, slot],
            device(x, y + step, z, core),
        )
        copy.start()
        started.append(copy)

    def y_forward(p):
        arrived(block(3, 0, p), b_recv.at[p, 0])
        y_go(3, 0, p, 4, 1)
        arrived(block(1, 1, p), b_recv.at[p, 3])
        y_go(1, 1, p, 5, 3)

    def lay_out(dy):
        at = (y + dy) % 4
        rows = pl.ds(pl.multiple_of(at * 512, 512), 512)
        for n in range(5):
            weights[rows, n * 128 : n * 128 + 128] = landed[
                at, :, n * 32 : n * 32 + 32, :
            ].reshape(512, 128)
        pairs = landed[at, :, 160:176, :]
        step_weights[rows, :] = jnp.concatenate(
            [pairs[:, :, :64], pairs[:, :, 64:]], axis=1
        ).reshape(512, 64)

    def columns(dk, dz, h):
        k = (y + dk) % 4
        return out_weights.at[k // 2, k % 2, (z + dz) % 4, h]

    def along(h, stage):
        return (h == 1) == (stage == 1)

    def unit(h, stage, unit_at, away):
        if along(h, stage):
            return columns(away, unit_at, h)
        return columns(unit_at, away, h)

    def o_go(h, stage, unit_at, away, slot, step, part=None):
        held = unit(h, stage, unit_at, away)
        if part is not None:
            held = held.at[pl.ds(part * 16, 16)]
        where = device(x, y + step, z, core) if along(h, stage) else device(x, y, z + step, core)
        index = (stage - 1) * 8 + unit_at * (stage - 1) * 4 + h * (4 if stage == 1 else 16) + slot
        copy = remote(held, held, o_send.at[index], o_recv.at[index], where)
        copy.start()
        started.append(copy)

    def o_wait(h, stage, unit_at, away, slot, part=None):
        held = unit(h, stage, unit_at, away)
        if part is not None:
            held = held.at[pl.ds(part * 16, 16)]
        index = (stage - 1) * 8 + unit_at * (stage - 1) * 4 + h * (4 if stage == 1 else 16) + slot
        arrived(held, o_recv.at[index])

    def o_both(h, stage, unit_at):
        o_go(h, stage, unit_at, 0, 0, 1)
        o_go(h, stage, unit_at, 0, 1, 3)

    def o_forward(h, stage, unit_at):
        o_wait(h, stage, unit_at, 3, 0)
        o_go(h, stage, unit_at, 3, 2, 1, 0)
        o_wait(h, stage, unit_at, 1, 1)
        o_go(h, stage, unit_at, 1, 3, 3, 1)

    def o_last(h, stage, unit_at):
        o_wait(h, stage, unit_at, 2, 2, 0)
        o_wait(h, stage, unit_at, 2, 3, 1)

    def o_begin():
        arrived(out_weights.at[y // 2, y % 2, z], w_sem.at[1])
        for h in range(2):
            o_both(h, 1, 0)
        for h in range(2):
            o_both(h, 2, 0)

    def o_second():
        for h in range(2):
            o_forward(h, 1, 0)
            o_both(h, 2, 3)
            o_both(h, 2, 1)

    def o_third():
        for h in range(2):
            o_last(h, 1, 0)
            o_both(h, 2, 2)
        for h in range(2):
            o_forward(h, 2, 0)

    def o_fourth():
        for h in range(2):
            o_forward(h, 2, 3)
            o_forward(h, 2, 1)

    def o_fifth():
        for h in range(2):
            o_forward(h, 2, 2)

    def o_end():
        for h in range(2):
            for unit_at in range(4):
                o_last(h, 2, unit_at)

    for p in range(2):
        arrived(landed.at[y, :, parts[p]], a_recv.at[p])
        y_go(0, 0, p, 0, 1)
        y_go(0, 1, p, 3, 3)
        y_go(0, 1, p, 1, 1)
        y_go(0, 0, p, 2, 3)

    for hi in range(2):
        arrived(quarter.at[1 - core, :, pl.ds(hi * 1024, 1024)], q_sem.at[2 + hi])
    sent_on = remote(
        quarter,
        out_weights.at[y // 2, y % 2, z],
        w_sem.at[0],
        w_sem.at[1],
        device(target_x, y, z, core),
    )
    kept = pltpu.make_async_copy(quarter, out_weights.at[y // 2, y % 2, z], w_sem.at[1])
    pl.when(jnp.logical_not(stays))(sent_on.start)
    pl.when(stays)(kept.start)

    arrived(piece(3, 0), z_recv.at[0])
    z_go(3, 0, 4, 1)
    x_go(3, 0, 1)
    arrived(piece(1, 1), z_recv.at[3])
    z_go(1, 1, 5, 3)
    x_go(1, 1, 2)
    y_forward(0)
    arrived(piece(3, 1), z_recv.at[1])
    x_go(3, 1, 1)
    arrived(piece(1, 0), z_recv.at[2])
    x_go(1, 0, 2)
    lay_out(0)
    arrived(other(3, 0), x_recv.at[2])
    z_go(3, 0, 6, 1, other)
    arrived(other(1, 1), x_recv.at[5])
    z_go(1, 1, 7, 3, other)
    y_forward(1)
    o_begin()

    arrived(block(3, 1, 0), b_recv.at[0, 1])
    arrived(block(3, 1, 1), b_recv.at[1, 1])
    lay_out(3)
    arrived(block(1, 0, 0), b_recv.at[0, 2])
    arrived(block(1, 0, 1), b_recv.at[1, 2])
    lay_out(1)
    arrived(piece(2, 0), z_recv.at[4])
    arrived(piece(2, 1), z_recv.at[5])
    arrived(other(0, 0), x_recv.at[0])
    arrived(other(0, 1), x_recv.at[1])
    arrived(other(3, 1), x_recv.at[3])
    arrived(other(1, 0), x_recv.at[4])

    for p in range(2):
        arrived(block(2, 0, p), b_recv.at[p, 4])
        arrived(block(2, 1, p), b_recv.at[p, 5])
    lay_out(2)
    arrived(other(2, 0), z_recv.at[6])
    arrived(other(2, 1), z_recv.at[7])

    def to_twin(i):
        return remote(give.at[i], got.at[i], d_send.at[i], d_recv.at[i], twin)

    step_half = jnp.dot(act[mine], step_weights[...], preferred_element_type=jnp.float32)
    step_give[...] = jnp.concatenate([step_half, step_half], axis=1)
    step_copy = remote(step_give, step_got, t_sem.at[0], t_sem.at[1], twin)
    step_copy.start()

    bc_slot = x_lo * 2 + z % 2
    has_bc = core == z // 2

    def bc_twin(i):
        two = pl.ds(i * 2, 2)
        return remote(shared.at[two], shared_got.at[two], g_send.at[i], g_recv.at[i], twin)

    def multiply_bc(i, carry):
        two = pl.ds(i * 2, 2)
        shared[two] = jnp.dot(
            act[two].reshape(256, 2048), weights[:, 512:], preferred_element_type=jnp.float32
        ).reshape(2, 128, 128)
        pl.when(jnp.logical_not(has_bc))(bc_twin(i).start)
        return carry

    lax.fori_loop(0, 4, multiply_bc, 0)

    def multiply(i, carry):
        product = jnp.dot(act[i], weights[:, :512], preferred_element_type=jnp.float32)
        first, second = product[:, :256], product[:, 256:]
        keep[i] = jnp.where(core == 0, first, second)
        give[i] = jnp.where(core == 0, second, first)
        to_twin(i).start()
        return carry

    def owner(i):
        return device(x_hi * 2 + i // 4, y, i % 4, core)

    def xz_far(i):
        return remote(rounded.at[i], xz.at[mine], r_send.at[i], r_recv.at[mine], owner(i))

    def bc_far(i):
        return remote(shared.at[i], bc.at[bc_slot], c_send.at[i], c_recv.at[bc_slot], owner(i))

    lax.fori_loop(0, 4, multiply, 0)
    o_second()

    @pl.when(has_bc)
    def _():
        for i in range(4):
            two = pl.ds(i * 2, 2)
            bc_twin(i).wait_recv()
            shared[two] = shared[two] + shared_got[two]

        def hand_out_bc(i, carry):
            pl.when(i != mine)(lambda: bc_far(i).start())

            @pl.when(i == mine)
            def _():
                pltpu.make_async_copy(
                    shared.at[i], bc.at[bc_slot], c_recv.at[bc_slot]
                ).start()

            return carry

        lax.fori_loop(0, 8, hand_out_bc, 0)

    lax.fori_loop(4, 8, multiply, 0)

    def hand_out(i, carry):
        to_twin(i).wait_recv()
        total = keep[i] + got[i]
        gate = total[:, 128:]
        rounded[i, :, :128] = total[:, :128].astype(jnp.bfloat16)
        rounded[i, :, 128:] = (gate / (1.0 + jnp.exp(-gate))).astype(jnp.bfloat16)
        pl.when(i != mine)(lambda: xz_far(i).start())

        @pl.when(i == mine)
        def _():
            pltpu.make_async_copy(rounded.at[i], xz.at[mine], r_recv.at[mine]).start()

        return carry

    lax.fori_loop(0, 8, hand_out, 0)
    o_third()

    step_copy.wait()
    step_sum = step_give[...] + step_got[...]
    step_raw = jnp.zeros((128, 16), jnp.float32)
    for t in range(4):
        step_raw += jnp.where(x_hi * 2 + core == t, step_sum[:, t * 16 : t * 16 + 16], 0.0)
    raw = step_raw + bias_ref[...]
    step_size = jnp.maximum(raw, 0.0) + jnp.log1p(jnp.exp(-jnp.abs(raw)))
    decay = jnp.exp(-jnp.exp(rate_ref[...]) * step_size)

    for slot in range(4):
        arrived(bc.at[slot], c_recv.at[slot])
    for copy in state_copies:
        copy.wait()

    def look(row, carry):
        steps_of = pl.ds(row, 4, stride=32)
        c_rows = jnp.concatenate([bc[2, steps_of, :], bc[3, steps_of, :]], axis=1)
        upper = c_rows.astype(jnp.bfloat16)
        lower = (c_rows - upper.astype(jnp.float32)).astype(jnp.bfloat16)
        seen = lax.dot_general(
            jnp.concatenate([upper, lower], axis=0),
            state[row],
            (((1,), (1,)), ((), ())),
            preferred_element_type=jnp.float32,
        )
        for t in range(4):
            read[pl.ds(t * 32 + row, 1), :] = seen[t : t + 1] + seen[t + 4 : t + 5]
        return carry

    lax.fori_loop(0, 16, look, 0, unroll=4)
    o_fourth()
    lax.fori_loop(16, 32, look, 0, unroll=4)
    o_fifth()

    at = [slice(t * 32, t * 32 + 32) for t in range(4)]
    b = jnp.concatenate([bc[0], bc[1]], axis=1)
    c = jnp.concatenate([bc[2], bc[3]], axis=1)
    rows, total, coefs = [], None, []
    for t in range(4):
        total = decay[at[t]] if t == 0 else total * decay[at[t]]
        coefs = [member * decay[at[t]] for member in coefs] + [step_size[at[t]]]
        rows.append(total)
        for s in range(t + 1):
            term = coefs[s] * jnp.sum(b[at[s]] * c[at[t]], axis=1, keepdims=True)
            rows.append(term + skip_ref[...] if s == t else term)
    table = jnp.concatenate(rows, axis=0)
    head = lax.broadcasted_iota(jnp.int32, (16, 1024), 0)
    channel = lax.broadcasted_iota(jnp.int32, (16, 1024), 1)
    spread = jnp.where(channel // 64 == head, 1.0, 0.0).astype(jnp.float32)
    wide = jnp.dot(
        table, spread, precision=lax.Precision.HIGHEST, preferred_element_type=jnp.float32
    )

    for j in range(8):
        arrived(xz.at[j], r_recv.at[j])

    def hid_part(block, away, part=None):
        rows_of = pl.ds(block * 64, 64) if part is None else pl.ds(block * 64 + part * 32, 32)
        return hid.at[(x + away) % 4, rows_of]

    def h_go(block, away, slot, step, part=None):
        held = hid_part(block, away, part)
        copy = remote(
            held, held, h_send.at[block, slot], h_recv.at[block, slot], device(x + step, y, z, core)
        )
        copy.start()
        started.append(copy)

    def h_forward(block):
        arrived(hid_part(block, 3), h_recv.at[block, 0])
        h_go(block, 3, 2, 1, 0)
        arrived(hid_part(block, 1), h_recv.at[block, 1])
        h_go(block, 1, 3, 3, 1)

    def h_last(block):
        arrived(hid_part(block, 2, 0), h_recv.at[block, 2])
        arrived(hid_part(block, 2, 1), h_recv.at[block, 3])

    for block in range(2):
        sixteen = [slice(t * 32 + block * 16, t * 32 + block * 16 + 16) for t in range(4)]
        xs = [
            jnp.concatenate([xz[j, sixteen[t], :128] for j in range(8)], axis=1).astype(
                jnp.float32
            )
            for t in range(4)
        ]
        k = block * 16
        for t in range(4):
            seen = wide[k : k + 16] * read[sixteen[t], :]
            k += 32
            for s in range(t + 1):
                seen += wide[k : k + 16] * xs[s]
                k += 32
            gate = jnp.concatenate([xz[j, sixteen[t], 128:] for j in range(8)], axis=1)
            gated = seen * gate.astype(jnp.float32)
            inv_rms = lax.rsqrt(jnp.mean(gated * gated, axis=1, keepdims=True) + eps)
            hid[x, block * 64 + t * 16 : block * 64 + t * 16 + 16, :] = (
                gated * inv_rms * gain_ref[...]
            ).astype(jnp.bfloat16)
        h_go(block, 0, 0, 1)
        h_go(block, 0, 1, 3)

    h_forward(0)
    h_last(0)
    h_forward(1)
    o_end()

    def against(left, right):
        return lax.dot_general(
            left, right, (((1,), (1,)), ((), ())), preferred_element_type=jnp.float32
        )

    def partial(block, which):
        held = out_weights[which].reshape(512, 2048)
        rows_of = slice(block * 64, block * 64 + 64)
        product = against(hid[0:2, rows_of].reshape(128, 1024), held[:, :1024]) + against(
            hid[2:4, rows_of].reshape(128, 1024), held[:, 1024:]
        )
        return product.reshape(2, 64, 512)

    theirs = 1 - x_lo

    def out_twin(block):
        return remote(
            out_give.at[block], out_got.at[block], e_send.at[block], e_recv.at[block], twin
        )

    def back_copy(block):
        return remote(
            back.at[block],
            theirs_in.at[:, pl.ds(block * 16, 16)],
            f_send.at[block],
            f_recv.at[block],
            device(x_hi * 2 + theirs, y, z, core),
        )

    def give_out(block):
        out_give[block] = partial(block, 1 - core)
        out_twin(block).start()

    def join(block):
        out_twin(block).wait_recv()
        back[block] = (out_keep[block, theirs] + out_got[block, theirs]).reshape(4, 16, 512)
        back_copy(block).start()
        ours[:, block * 16 : block * 16 + 16] = (
            out_keep[block, x_lo] + out_got[block, x_lo]
        ).reshape(4, 16, 512)

    give_out(0)
    out_keep[0] = partial(0, core)
    h_last(1)
    give_out(1)
    join(0)
    out_keep[1] = partial(1, core)
    join(1)

    for copy in started:
        copy.wait_send()
    pl.when(jnp.logical_not(stays))(sent_on.wait_send)

    def sent(i, carry):
        to_twin(i).wait_send()

        @pl.when(i != mine)
        def _():
            xz_far(i).wait_send()
            pl.when(has_bc)(bc_far(i).wait_send)

        return carry

    lax.fori_loop(0, 8, sent, 0)

    @pl.when(jnp.logical_not(has_bc))
    def _():
        for i in range(4):
            bc_twin(i).wait_send()

    for block in range(2):
        out_twin(block).wait_send()
        back_copy(block).wait_send()
        rows_of = pl.ds(block * 16, 16)
        arrived(theirs_in.at[:, rows_of], f_recv.at[block])
        first = jnp.where(x_lo == 0, ours[:, rows_of], theirs_in[:, rows_of])
        second = jnp.where(x_lo == 0, theirs_in[:, rows_of], ours[:, rows_of])
        for j in range(8):
            span = slice(j * 64, j * 64 + 64)
            mix = jnp.concatenate([first[:, :, span], second[:, :, span]], axis=2)
            lanes = pl.ds(pl.multiple_of((x_hi * 2 + core) * 1024 + j * 128, 128), 128)
            for t in range(4):
                residual = act_ref[t * 32 + block * 16 : t * 32 + block * 16 + 16, lanes].astype(
                    jnp.float32
                )
                active = length_ref[block * 16 : block * 16 + 16] > t
                out_ref[t, rows_of, j * 128 : j * 128 + 128] = jnp.where(
                    active, residual + mix[t], residual
                ).astype(jnp.bfloat16)


def mixer(weight_x, weight_z, weight_b, weight_c, weight_step, flat_in, out_weight, log_rate, step_bias, skip_gain, norm_gain, lengths, state):
    dma = pltpu.SemaphoreType.DMA
    vmem = pl.BlockSpec(memory_space=pltpu.VMEM)
    bf16, f32 = jnp.bfloat16, jnp.float32
    return pl.pallas_call(
        mixer_kernel,
        out_shape=jax.ShapeDtypeStruct((4, 32, 1024), bf16),
        in_specs=[vmem] * 12 + [pl.BlockSpec(memory_space=pl.ANY)],
        out_specs=vmem,
        scratch_shapes=[
            pltpu.VMEM((16, 176, 128), bf16),
            pltpu.VMEM((8, 128, 2048), bf16),
            pltpu.VMEM((4, 16, 176, 128), bf16),
            pltpu.VMEM((2048, 640), bf16),
            pltpu.VMEM((2048, 64), bf16),
            pltpu.VMEM((8, 128, 256), f32),
            pltpu.VMEM((8, 128, 256), f32),
            pltpu.VMEM((8, 128, 256), f32),
            pltpu.VMEM((8, 128, 256), bf16),
            pltpu.VMEM((8, 128, 128), f32),
            pltpu.VMEM((8, 128, 128), f32),
            pltpu.VMEM((8, 128, 256), bf16),
            pltpu.VMEM((4, 128, 128), f32),
            pltpu.VMEM((128, 128), f32),
            pltpu.VMEM((128, 128), f32),
            pltpu.VMEM((32, 1024, 256), bf16),
            pltpu.VMEM((128, 1024), f32),
            pltpu.VMEM((2, 32, 2048), bf16),
            pltpu.VMEM((2, 2, 4, 2, 32, 2048), bf16),
            pltpu.VMEM((4, 128, 1024), bf16),
            pltpu.VMEM((2, 2, 64, 512), f32),
            pltpu.VMEM((2, 2, 64, 512), f32),
            pltpu.VMEM((2, 2, 64, 512), f32),
            pltpu.VMEM((2, 4, 16, 512), f32),
            pltpu.VMEM((4, 32, 512), f32),
            pltpu.VMEM((4, 32, 512), f32),
            dma((4,)),
            dma((4,)),
            dma((4,)),
            dma((2, 15)),
            dma((2,)),
            dma((2, 6)),
            dma((2, 6)),
            dma((8,)),
            dma((8,)),
            dma((6,)),
            dma((6,)),
            dma((8,)),
            dma((8,)),
            dma((8,)),
            dma((8,)),
            dma((8,)),
            dma((4,)),
            dma((2,)),
            dma((4,)),
            dma((2,)),
            dma((40,)),
            dma((40,)),
            dma((2, 4)),
            dma((2, 4)),
            dma((2,)),
            dma((2,)),
            dma((2,)),
            dma((2,)),
        ],
        compiler_params=pltpu.CompilerParams(
            collective_id=0, has_side_effects=True, vmem_limit_bytes=58 << 20
        ),
        cost_estimate=pl.CostEstimate(
            flops=4 << 30, bytes_accessed=200 << 20, transcendentals=0
        ),
        name="mixer",
    )(
        weight_x,
        weight_z,
        weight_b,
        weight_c,
        weight_step,
        flat_in,
        out_weight,
        log_rate.reshape(1, 16),
        step_bias.reshape(1, 16),
        skip_gain.reshape(1, 16),
        norm_gain.reshape(1, 1024),
        lengths.reshape(32, 1),
        state,
    )


def shards(
    layer_in,
    lengths,
    prior_state,
    weight_x,
    weight_z,
    weight_b,
    weight_c,
    weight_step,
    weight_out,
    log_rate,
    step_bias,
    skip_gain,
    norm_gain,
):
    flat_in = layer_in.reshape(128, 4096)

    return mixer(
        weight_x,
        weight_z,
        weight_b,
        weight_c,
        weight_step,
        flat_in,
        weight_out.T,
        log_rate,
        step_bias,
        skip_gain,
        norm_gain,
        lengths,
        prior_state.reshape(32, 1024, 256),
    )


def solution(mesh):
    placed = (
        P(None, "group", None),
        P("group"),
        P("group", "tensor", None, None),
        P(("group", "tensor"), None),
        P(("group", "tensor"), None),
        P(("group", "tensor"), None),
        P(("group", "tensor"), None),
        P(("group", "tensor"), None),
        P(None, ("group", "tensor")),
        P("tensor"),
        P("tensor"),
        P("tensor"),
        P("tensor"),
    )
    return jax.shard_map(
        shards, mesh=mesh, in_specs=placed, out_specs=P(None, "group", "tensor"), check_vma=False
    )
```

```python
import jax
import jax.numpy as jnp
from jax import lax
from jax.experimental import pallas as pl
from jax.experimental.pallas import tpu as pltpu
from jax.sharding import PartitionSpec as P

MESH = pl.DeviceIdType.MESH
eps = 1e-05


def here():
    group, tensor = lax.axis_index("group"), lax.axis_index("tensor")
    return (tensor // 2) * 2 + group // 16, (group // 4) % 4, group % 4, tensor % 2


def device(x, y, z, core):
    return ((x % 2) * 16 + (y % 4) * 4 + z % 4, ((x % 4) // 2) * 2 + core % 2)


def remote(source, target, send_sem, recv_sem, where):
    return pltpu.make_async_remote_copy(
        src_ref=source,
        dst_ref=target,
        send_sem=send_sem,
        recv_sem=recv_sem,
        device_id=where,
        device_id_type=MESH,
    )


def arrived(ref, sem):
    pltpu.make_async_copy(ref, ref, sem).wait()


TURNS = (1, 3, 2)


def mixer_kernel(
    x_ref,
    z_ref,
    b_ref,
    c_ref,
    fold_ref,
    act_ref,
    out_weight_ref,
    rate_ref,
    bias_ref,
    skip_ref,
    gain_ref,
    length_ref,
    state_ref,
    out_ref,
    pack,
    act,
    landed,
    weights,
    step_weights,
    keep,
    give,
    got,
    rounded,
    shared,
    shared_got,
    xz,
    bc,
    step_give,
    step_got,
    state,
    read,
    quarter,
    out_weights,
    hid,
    out_keep,
    out_give,
    out_got,
    back,
    ours,
    theirs_in,
    s_sem,
    g_send,
    g_recv,
    a_send,
    a_recv,
    b_send,
    b_recv,
    z_send,
    z_recv,
    x_send,
    x_recv,
    d_send,
    d_recv,
    r_send,
    r_recv,
    c_send,
    c_recv,
    t_sem,
    q_sem,
    w_sem,
    o_send,
    o_recv,
    h_send,
    h_recv,
    e_send,
    e_recv,
    f_send,
    f_recv,
):
    x, y, z, core = here()
    x_lo, x_hi = x % 2, x // 2
    mine = x_lo * 4 + z
    twin = device(x, y, z, core + 1)
    started = []

    target_x = x_lo * 2 + x_hi
    stays = target_x == x

    barrier = pltpu.get_barrier_semaphore()

    def signal(where):
        pl.semaphore_signal(barrier, inc=1, device_id=where, device_id_type=MESH)

    plane = [(dx, dz) for dz in (2, 1, 3, 0) for dx in (2, 1, 3, 0)]
    for dx, dz in plane[:-1]:
        signal(device(x + dx, y, z + dz, core))
    for step in TURNS:
        signal(device(x, y + step, z, core))
    signal(twin)
    pl.when(jnp.logical_not(stays))(lambda: signal(device(target_x, y, z, core)))

    lane = lax.broadcasted_iota(jnp.int32, (256, 128), 1)
    from_lane = lax.broadcasted_iota(jnp.int32, (256, 128), 0)
    chosen = from_lane == (lane // 32) * 64 + core * 32 + lane % 32
    picker = jnp.where(chosen, 1.0, 0.0).astype(jnp.bfloat16)
    for i in range(16):
        spot = ((i % 8) // 2) * 4 + (i // 8) * 2 + i % 2
        act[mine, :, spot * 128 : spot * 128 + 128] = jnp.dot(
            act_ref[:, i * 256 : i * 256 + 256], picker, preferred_element_type=jnp.float32
        ).astype(jnp.bfloat16)

    fold = jnp.concatenate([fold_ref[:16], fold_ref[16:]], axis=1)
    for hi in range(2):
        for j in range(8):
            to = hi * 8 + j
            for half in range(2):
                lanes = slice((hi * 16 + half * 8 + j) * 128, (hi * 16 + half * 8 + j + 1) * 128)
                pack[to, half * 64 : half * 64 + 32] = x_ref[:, lanes]
                pack[to, half * 64 + 32 : half * 64 + 64] = z_ref[:, lanes]
            lanes = slice((hi * 4 + j % 4) * 128, (hi * 4 + j % 4 + 1) * 128)
            pack[to, 128:160] = (b_ref if j < 4 else c_ref)[:, lanes]
            pack[to, 160:176] = fold
    for hi in range(2):
        quarter[core, :, hi * 1024 : hi * 1024 + 1024] = out_weight_ref[
            :, pl.ds(pl.multiple_of((hi * 2 + core) * 1024, 1024), 1024)
        ]

    pl.semaphore_wait(barrier, 20 - jnp.where(stays, 1, 0))

    parts = (pl.ds(0, 96), pl.ds(96, 80))
    landing = landed.at[y, x_lo * 8 + z * 2 + x_hi]
    for p in range(2):
        for n, (dx, dz) in enumerate(plane):
            xd, zd = (x + dx) % 4, (z + dz) % 4
            tile = pack.at[(xd // 2) * 8 + (xd % 2) * 4 + zd, parts[p]]
            to = landing.at[parts[p]]
            if n == 15:
                pltpu.make_async_copy(tile, to, a_recv.at[p]).start()
            else:
                copy = remote(tile, to, a_send.at[p, n], a_recv.at[p], device(xd, y, zd, core))
                copy.start()
                started.append(copy)

    def piece(dz, h):
        return act.at[x_lo * 4 + (z + dz) % 4, pl.ds(h * 64, 64)]

    def other(dz, h):
        return act.at[(1 - x_lo) * 4 + (z + dz) % 4, pl.ds(h * 64, 64)]

    def z_go(dz, h, slot, step, ref=piece):
        copy = remote(
            ref(dz, h),
            ref(dz, h),
            z_send.at[slot],
            z_recv.at[slot],
            device(x, y, z + step, core),
        )
        copy.start()
        started.append(copy)

    def x_go(dz, h, rel):
        slot = rel * 2 + h
        copy = remote(
            piece(dz, h),
            piece(dz, h),
            x_send.at[slot],
            x_recv.at[slot],
            device(x + (1 if h == 0 else 3), y, z, core),
        )
        copy.start()
        started.append(copy)

    z_go(0, 0, 0, 1)
    z_go(0, 1, 3, 3)
    x_go(0, 0, 0)
    x_go(0, 1, 0)
    z_go(0, 1, 1, 1)
    z_go(0, 0, 2, 3)

    for hi in range(2):
        copy = remote(
            out_weight_ref.at[:, pl.ds(pl.multiple_of((hi * 2 + 1 - core) * 1024, 1024), 1024)],
            quarter.at[core, :, pl.ds(hi * 1024, 1024)],
            q_sem.at[hi],
            q_sem.at[2 + hi],
            twin,
        )
        copy.start()
        started.append(copy)

    state_copies = [
        pltpu.make_async_copy(
            state_ref.at[pl.ds(n * 8, 8)], state.at[pl.ds(n * 8, 8)], s_sem.at[n]
        )
        for n in range(4)
    ]
    for copy in state_copies:
        copy.start()

    def block(dy, h, p):
        return landed.at[(y + dy) % 4, pl.ds(h * 8, 8), parts[p]]

    def y_go(dy, h, p, slot, step):
        copy = remote(
            block(dy, h, p),
            block(dy, h, p),
            b_send.at[p, slot],
            b_recv.at[p, slot],
            device(x, y + step, z, core),
        )
        copy.start()
        started.append(copy)

    def y_forward(p):
        arrived(block(3, 0, p), b_recv.at[p, 0])
        y_go(3, 0, p, 4, 1)
        arrived(block(1, 1, p), b_recv.at[p, 3])
        y_go(1, 1, p, 5, 3)

    def lay_out(dy):
        at = (y + dy) % 4
        rows = pl.ds(pl.multiple_of(at * 512, 512), 512)
        for n in range(5):
            weights[rows, n * 128 : n * 128 + 128] = landed[
                at, :, n * 32 : n * 32 + 32, :
            ].reshape(512, 128)
        pairs = landed[at, :, 160:176, :]
        step_weights[rows, :] = jnp.concatenate(
            [pairs[:, :, :64], pairs[:, :, 64:]], axis=1
        ).reshape(512, 64)

    def columns(dk, dz, h):
        k = (y + dk) % 4
        return out_weights.at[k // 2, k % 2, (z + dz) % 4, h]

    def along(h, stage):
        return (h == 1) == (stage == 1)

    def unit(h, stage, unit_at, away):
        if along(h, stage):
            return columns(away, unit_at, h)
        return columns(unit_at, away, h)

    def o_go(h, stage, unit_at, away, slot, step, part=None):
        held = unit(h, stage, unit_at, away)
        if part is not None:
            held = held.at[pl.ds(part * 16, 16)]
        where = device(x, y + step, z, core) if along(h, stage) else device(x, y, z + step, core)
        index = (stage - 1) * 8 + unit_at * (stage - 1) * 4 + h * (4 if stage == 1 else 16) + slot
        copy = remote(held, held, o_send.at[index], o_recv.at[index], where)
        copy.start()
        started.append(copy)

    def o_wait(h, stage, unit_at, away, slot, part=None):
        held = unit(h, stage, unit_at, away)
        if part is not None:
            held = held.at[pl.ds(part * 16, 16)]
        index = (stage - 1) * 8 + unit_at * (stage - 1) * 4 + h * (4 if stage == 1 else 16) + slot
        arrived(held, o_recv.at[index])

    def o_both(h, stage, unit_at):
        o_go(h, stage, unit_at, 0, 0, 1)
        o_go(h, stage, unit_at, 0, 1, 3)

    def o_forward(h, stage, unit_at):
        o_wait(h, stage, unit_at, 3, 0)
        o_go(h, stage, unit_at, 3, 2, 1, 0)
        o_wait(h, stage, unit_at, 1, 1)
        o_go(h, stage, unit_at, 1, 3, 3, 1)

    def o_last(h, stage, unit_at):
        o_wait(h, stage, unit_at, 2, 2, 0)
        o_wait(h, stage, unit_at, 2, 3, 1)

    def o_begin():
        arrived(out_weights.at[y // 2, y % 2, z], w_sem.at[1])
        for h in range(2):
            o_both(h, 1, 0)
        for h in range(2):
            o_both(h, 2, 0)

    def o_second():
        for h in range(2):
            o_forward(h, 1, 0)
            o_both(h, 2, 3)
            o_both(h, 2, 1)

    def o_third():
        for h in range(2):
            o_last(h, 1, 0)
            o_both(h, 2, 2)
        for h in range(2):
            o_forward(h, 2, 0)

    def o_fourth():
        for h in range(2):
            o_forward(h, 2, 3)
            o_forward(h, 2, 1)

    def o_fifth():
        for h in range(2):
            o_forward(h, 2, 2)

    def o_end():
        for h in range(2):
            for unit_at in range(4):
                o_last(h, 2, unit_at)

    for p in range(2):
        arrived(landed.at[y, :, parts[p]], a_recv.at[p])
        y_go(0, 0, p, 0, 1)
        y_go(0, 1, p, 3, 3)
        y_go(0, 1, p, 1, 1)
        y_go(0, 0, p, 2, 3)

    for hi in range(2):
        arrived(quarter.at[1 - core, :, pl.ds(hi * 1024, 1024)], q_sem.at[2 + hi])
    sent_on = remote(
        quarter,
        out_weights.at[y // 2, y % 2, z],
        w_sem.at[0],
        w_sem.at[1],
        device(target_x, y, z, core),
    )
    kept = pltpu.make_async_copy(quarter, out_weights.at[y // 2, y % 2, z], w_sem.at[1])
    pl.when(jnp.logical_not(stays))(sent_on.start)
    pl.when(stays)(kept.start)

    arrived(piece(3, 0), z_recv.at[0])
    z_go(3, 0, 4, 1)
    x_go(3, 0, 1)
    arrived(piece(1, 1), z_recv.at[3])
    z_go(1, 1, 5, 3)
    x_go(1, 1, 2)
    y_forward(0)
    arrived(piece(3, 1), z_recv.at[1])
    x_go(3, 1, 1)
    arrived(piece(1, 0), z_recv.at[2])
    x_go(1, 0, 2)
    lay_out(0)
    arrived(other(3, 0), x_recv.at[2])
    z_go(3, 0, 6, 1, other)
    arrived(other(1, 1), x_recv.at[5])
    z_go(1, 1, 7, 3, other)
    y_forward(1)
    o_begin()

    arrived(block(3, 1, 0), b_recv.at[0, 1])
    arrived(block(3, 1, 1), b_recv.at[1, 1])
    lay_out(3)
    arrived(block(1, 0, 0), b_recv.at[0, 2])
    arrived(block(1, 0, 1), b_recv.at[1, 2])
    lay_out(1)
    arrived(piece(2, 0), z_recv.at[4])
    arrived(piece(2, 1), z_recv.at[5])
    arrived(other(0, 0), x_recv.at[0])
    arrived(other(0, 1), x_recv.at[1])
    arrived(other(3, 1), x_recv.at[3])
    arrived(other(1, 0), x_recv.at[4])

    for p in range(2):
        arrived(block(2, 0, p), b_recv.at[p, 4])
        arrived(block(2, 1, p), b_recv.at[p, 5])
    lay_out(2)
    arrived(other(2, 0), z_recv.at[6])
    arrived(other(2, 1), z_recv.at[7])

    def to_twin(i):
        return remote(give.at[i], got.at[i], d_send.at[i], d_recv.at[i], twin)

    step_half = jnp.dot(act[mine], step_weights[...], preferred_element_type=jnp.float32)
    step_give[...] = jnp.concatenate([step_half, step_half], axis=1)
    step_copy = remote(step_give, step_got, t_sem.at[0], t_sem.at[1], twin)
    step_copy.start()

    bc_slot = x_lo * 2 + z % 2
    has_bc = core == z // 2

    def bc_twin(i):
        two = pl.ds(i * 2, 2)
        return remote(shared.at[two], shared_got.at[two], g_send.at[i], g_recv.at[i], twin)

    def multiply_bc(i, carry):
        two = pl.ds(i * 2, 2)
        shared[two] = jnp.dot(
            act[two].reshape(256, 2048), weights[:, 512:], preferred_element_type=jnp.float32
        ).reshape(2, 128, 128)
        pl.when(jnp.logical_not(has_bc))(bc_twin(i).start)
        return carry

    lax.fori_loop(0, 4, multiply_bc, 0)
    o_second()

    def multiply(i, carry):
        product = jnp.dot(act[i], weights[:, :512], preferred_element_type=jnp.float32)
        first, second = product[:, :256], product[:, 256:]
        keep[i] = jnp.where(core == 0, first, second)
        give[i] = jnp.where(core == 0, second, first)
        to_twin(i).start()
        return carry

    def owner(i):
        return device(x_hi * 2 + i // 4, y, i % 4, core)

    def xz_far(i):
        return remote(rounded.at[i], xz.at[mine], r_send.at[i], r_recv.at[mine], owner(i))

    def bc_far(i):
        return remote(shared.at[i], bc.at[bc_slot], c_send.at[i], c_recv.at[bc_slot], owner(i))

    lax.fori_loop(0, 4, multiply, 0)

    @pl.when(has_bc)
    def _():
        for i in range(4):
            two = pl.ds(i * 2, 2)
            bc_twin(i).wait_recv()
            shared[two] = shared[two] + shared_got[two]

        def hand_out_bc(i, carry):
            pl.when(i != mine)(lambda: bc_far(i).start())

            @pl.when(i == mine)
            def _():
                pltpu.make_async_copy(
                    shared.at[i], bc.at[bc_slot], c_recv.at[bc_slot]
                ).start()

            return carry

        lax.fori_loop(0, 8, hand_out_bc, 0)

    lax.fori_loop(4, 8, multiply, 0)
    o_third()

    def hand_out(i, carry):
        to_twin(i).wait_recv()
        total = keep[i] + got[i]
        gate = total[:, 128:]
        rounded[i, :, :128] = total[:, :128].astype(jnp.bfloat16)
        rounded[i, :, 128:] = (gate / (1.0 + jnp.exp(-gate))).astype(jnp.bfloat16)
        pl.when(i != mine)(lambda: xz_far(i).start())

        @pl.when(i == mine)
        def _():
            pltpu.make_async_copy(rounded.at[i], xz.at[mine], r_recv.at[mine]).start()

        return carry

    lax.fori_loop(0, 8, hand_out, 0)
    o_fourth()

    step_copy.wait()
    step_sum = step_give[...] + step_got[...]
    step_raw = jnp.zeros((128, 16), jnp.float32)
    for t in range(4):
        step_raw += jnp.where(x_hi * 2 + core == t, step_sum[:, t * 16 : t * 16 + 16], 0.0)
    raw = step_raw + bias_ref[...]
    step_size = jnp.maximum(raw, 0.0) + jnp.log1p(jnp.exp(-jnp.abs(raw)))
    decay = jnp.exp(-jnp.exp(rate_ref[...]) * step_size)

    for slot in range(4):
        arrived(bc.at[slot], c_recv.at[slot])
    for copy in state_copies:
        copy.wait()

    def look(row, carry):
        steps_of = pl.ds(row, 4, stride=32)
        c_rows = jnp.concatenate([bc[2, steps_of, :], bc[3, steps_of, :]], axis=1)
        upper = c_rows.astype(jnp.bfloat16)
        lower = (c_rows - upper.astype(jnp.float32)).astype(jnp.bfloat16)
        seen = lax.dot_general(
            jnp.concatenate([upper, lower], axis=0),
            state[row],
            (((1,), (1,)), ((), ())),
            preferred_element_type=jnp.float32,
        )
        for t in range(4):
            read[pl.ds(t * 32 + row, 1), :] = seen[t : t + 1] + seen[t + 4 : t + 5]
        return carry

    lax.fori_loop(0, 16, look, 0, unroll=4)
    o_fifth()
    lax.fori_loop(16, 32, look, 0, unroll=4)

    at = [slice(t * 32, t * 32 + 32) for t in range(4)]
    b = jnp.concatenate([bc[0], bc[1]], axis=1)
    c = jnp.concatenate([bc[2], bc[3]], axis=1)
    rows, total, coefs = [], None, []
    for t in range(4):
        total = decay[at[t]] if t == 0 else total * decay[at[t]]
        coefs = [member * decay[at[t]] for member in coefs] + [step_size[at[t]]]
        rows.append(total)
        for s in range(t + 1):
            term = coefs[s] * jnp.sum(b[at[s]] * c[at[t]], axis=1, keepdims=True)
            rows.append(term + skip_ref[...] if s == t else term)
    table = jnp.concatenate(rows, axis=0)
    head = lax.broadcasted_iota(jnp.int32, (16, 1024), 0)
    channel = lax.broadcasted_iota(jnp.int32, (16, 1024), 1)
    spread = jnp.where(channel // 64 == head, 1.0, 0.0).astype(jnp.float32)
    wide = jnp.dot(
        table, spread, precision=lax.Precision.HIGHEST, preferred_element_type=jnp.float32
    )

    for j in range(8):
        arrived(xz.at[j], r_recv.at[j])

    def hid_part(block, away, part=None):
        rows_of = pl.ds(block * 64, 64) if part is None else pl.ds(block * 64 + part * 32, 32)
        return hid.at[(x + away) % 4, rows_of]

    def h_go(block, away, slot, step, part=None):
        held = hid_part(block, away, part)
        copy = remote(
            held, held, h_send.at[block, slot], h_recv.at[block, slot], device(x + step, y, z, core)
        )
        copy.start()
        started.append(copy)

    def h_forward(block):
        arrived(hid_part(block, 3), h_recv.at[block, 0])
        h_go(block, 3, 2, 1, 0)
        arrived(hid_part(block, 1), h_recv.at[block, 1])
        h_go(block, 1, 3, 3, 1)

    def h_last(block):
        arrived(hid_part(block, 2, 0), h_recv.at[block, 2])
        arrived(hid_part(block, 2, 1), h_recv.at[block, 3])

    for block in range(2):
        sixteen = [slice(t * 32 + block * 16, t * 32 + block * 16 + 16) for t in range(4)]
        xs = [
            jnp.concatenate([xz[j, sixteen[t], :128] for j in range(8)], axis=1).astype(
                jnp.float32
            )
            for t in range(4)
        ]
        k = block * 16
        for t in range(4):
            seen = wide[k : k + 16] * read[sixteen[t], :]
            k += 32
            for s in range(t + 1):
                seen += wide[k : k + 16] * xs[s]
                k += 32
            gate = jnp.concatenate([xz[j, sixteen[t], 128:] for j in range(8)], axis=1)
            gated = seen * gate.astype(jnp.float32)
            inv_rms = lax.rsqrt(jnp.mean(gated * gated, axis=1, keepdims=True) + eps)
            hid[x, block * 64 + t * 16 : block * 64 + t * 16 + 16, :] = (
                gated * inv_rms * gain_ref[...]
            ).astype(jnp.bfloat16)
        h_go(block, 0, 0, 1)
        h_go(block, 0, 1, 3)

    h_forward(0)
    h_last(0)
    h_forward(1)
    o_end()

    def against(left, right):
        return lax.dot_general(
            left, right, (((1,), (1,)), ((), ())), preferred_element_type=jnp.float32
        )

    def partial(block, which):
        held = out_weights[which].reshape(512, 2048)
        rows_of = slice(block * 64, block * 64 + 64)
        product = against(hid[0:2, rows_of].reshape(128, 1024), held[:, :1024]) + against(
            hid[2:4, rows_of].reshape(128, 1024), held[:, 1024:]
        )
        return product.reshape(2, 64, 512)

    theirs = 1 - x_lo

    def out_twin(block):
        return remote(
            out_give.at[block], out_got.at[block], e_send.at[block], e_recv.at[block], twin
        )

    def back_copy(block):
        return remote(
            back.at[block],
            theirs_in.at[:, pl.ds(block * 16, 16)],
            f_send.at[block],
            f_recv.at[block],
            device(x_hi * 2 + theirs, y, z, core),
        )

    def give_out(block):
        out_give[block] = partial(block, 1 - core)
        out_twin(block).start()

    def join(block):
        out_twin(block).wait_recv()
        back[block] = (out_keep[block, theirs] + out_got[block, theirs]).reshape(4, 16, 512)
        back_copy(block).start()
        ours[:, block * 16 : block * 16 + 16] = (
            out_keep[block, x_lo] + out_got[block, x_lo]
        ).reshape(4, 16, 512)

    give_out(0)
    out_keep[0] = partial(0, core)
    h_last(1)
    give_out(1)
    join(0)
    out_keep[1] = partial(1, core)
    join(1)

    for copy in started:
        copy.wait_send()
    pl.when(jnp.logical_not(stays))(sent_on.wait_send)

    def sent(i, carry):
        to_twin(i).wait_send()

        @pl.when(i != mine)
        def _():
            xz_far(i).wait_send()
            pl.when(has_bc)(bc_far(i).wait_send)

        return carry

    lax.fori_loop(0, 8, sent, 0)

    @pl.when(jnp.logical_not(has_bc))
    def _():
        for i in range(4):
            bc_twin(i).wait_send()

    for block in range(2):
        out_twin(block).wait_send()
        back_copy(block).wait_send()
        rows_of = pl.ds(block * 16, 16)
        arrived(theirs_in.at[:, rows_of], f_recv.at[block])
        first = jnp.where(x_lo == 0, ours[:, rows_of], theirs_in[:, rows_of])
        second = jnp.where(x_lo == 0, theirs_in[:, rows_of], ours[:, rows_of])
        for j in range(8):
            span = slice(j * 64, j * 64 + 64)
            mix = jnp.concatenate([first[:, :, span], second[:, :, span]], axis=2)
            lanes = pl.ds(pl.multiple_of((x_hi * 2 + core) * 1024 + j * 128, 128), 128)
            for t in range(4):
                residual = act_ref[t * 32 + block * 16 : t * 32 + block * 16 + 16, lanes].astype(
                    jnp.float32
                )
                active = length_ref[block * 16 : block * 16 + 16] > t
                out_ref[t, rows_of, j * 128 : j * 128 + 128] = jnp.where(
                    active, residual + mix[t], residual
                ).astype(jnp.bfloat16)


def mixer(weight_x, weight_z, weight_b, weight_c, weight_step, flat_in, out_weight, log_rate, step_bias, skip_gain, norm_gain, lengths, state):
    dma = pltpu.SemaphoreType.DMA
    vmem = pl.BlockSpec(memory_space=pltpu.VMEM)
    bf16, f32 = jnp.bfloat16, jnp.float32
    return pl.pallas_call(
        mixer_kernel,
        out_shape=jax.ShapeDtypeStruct((4, 32, 1024), bf16),
        in_specs=[vmem] * 12 + [pl.BlockSpec(memory_space=pl.ANY)],
        out_specs=vmem,
        scratch_shapes=[
            pltpu.VMEM((16, 176, 128), bf16),
            pltpu.VMEM((8, 128, 2048), bf16),
            pltpu.VMEM((4, 16, 176, 128), bf16),
            pltpu.VMEM((2048, 640), bf16),
            pltpu.VMEM((2048, 64), bf16),
            pltpu.VMEM((8, 128, 256), f32),
            pltpu.VMEM((8, 128, 256), f32),
            pltpu.VMEM((8, 128, 256), f32),
            pltpu.VMEM((8, 128, 256), bf16),
            pltpu.VMEM((8, 128, 128), f32),
            pltpu.VMEM((8, 128, 128), f32),
            pltpu.VMEM((8, 128, 256), bf16),
            pltpu.VMEM((4, 128, 128), f32),
            pltpu.VMEM((128, 128), f32),
            pltpu.VMEM((128, 128), f32),
            pltpu.VMEM((32, 1024, 256), bf16),
            pltpu.VMEM((128, 1024), f32),
            pltpu.VMEM((2, 32, 2048), bf16),
            pltpu.VMEM((2, 2, 4, 2, 32, 2048), bf16),
            pltpu.VMEM((4, 128, 1024), bf16),
            pltpu.VMEM((2, 2, 64, 512), f32),
            pltpu.VMEM((2, 2, 64, 512), f32),
            pltpu.VMEM((2, 2, 64, 512), f32),
            pltpu.VMEM((2, 4, 16, 512), f32),
            pltpu.VMEM((4, 32, 512), f32),
            pltpu.VMEM((4, 32, 512), f32),
            dma((4,)),
            dma((4,)),
            dma((4,)),
            dma((2, 15)),
            dma((2,)),
            dma((2, 6)),
            dma((2, 6)),
            dma((8,)),
            dma((8,)),
            dma((6,)),
            dma((6,)),
            dma((8,)),
            dma((8,)),
            dma((8,)),
            dma((8,)),
            dma((8,)),
            dma((4,)),
            dma((2,)),
            dma((4,)),
            dma((2,)),
            dma((40,)),
            dma((40,)),
            dma((2, 4)),
            dma((2, 4)),
            dma((2,)),
            dma((2,)),
            dma((2,)),
            dma((2,)),
        ],
        compiler_params=pltpu.CompilerParams(
            collective_id=0, has_side_effects=True, vmem_limit_bytes=58 << 20
        ),
        cost_estimate=pl.CostEstimate(
            flops=4 << 30, bytes_accessed=200 << 20, transcendentals=0
        ),
        name="mixer",
    )(
        weight_x,
        weight_z,
        weight_b,
        weight_c,
        weight_step,
        flat_in,
        out_weight,
        log_rate.reshape(1, 16),
        step_bias.reshape(1, 16),
        skip_gain.reshape(1, 16),
        norm_gain.reshape(1, 1024),
        lengths.reshape(32, 1),
        state,
    )


def shards(
    layer_in,
    lengths,
    prior_state,
    weight_x,
    weight_z,
    weight_b,
    weight_c,
    weight_step,
    weight_out,
    log_rate,
    step_bias,
    skip_gain,
    norm_gain,
):
    flat_in = layer_in.reshape(128, 4096)

    return mixer(
        weight_x,
        weight_z,
        weight_b,
        weight_c,
        weight_step,
        flat_in,
        weight_out.T,
        log_rate,
        step_bias,
        skip_gain,
        norm_gain,
        lengths,
        prior_state.reshape(32, 1024, 256),
    )


def solution(mesh):
    placed = (
        P(None, "group", None),
        P("group"),
        P("group", "tensor", None, None),
        P(("group", "tensor"), None),
        P(("group", "tensor"), None),
        P(("group", "tensor"), None),
        P(("group", "tensor"), None),
        P(("group", "tensor"), None),
        P(None, ("group", "tensor")),
        P("tensor"),
        P("tensor"),
        P("tensor"),
        P("tensor"),
    )
    return jax.shard_map(
        shards, mesh=mesh, in_specs=placed, out_specs=P(None, "group", "tensor"), check_vma=False
    )
```

```python
import jax
import jax.numpy as jnp
from jax import lax
from jax.experimental import pallas as pl
from jax.experimental.pallas import tpu as pltpu
from jax.sharding import PartitionSpec as P

MESH = pl.DeviceIdType.MESH
eps = 1e-05


def here():
    group, tensor = lax.axis_index("group"), lax.axis_index("tensor")
    return (tensor // 2) * 2 + group // 16, (group // 4) % 4, group % 4, tensor % 2


def device(x, y, z, core):
    return ((x % 2) * 16 + (y % 4) * 4 + z % 4, ((x % 4) // 2) * 2 + core % 2)


def remote(source, target, send_sem, recv_sem, where):
    return pltpu.make_async_remote_copy(
        src_ref=source,
        dst_ref=target,
        send_sem=send_sem,
        recv_sem=recv_sem,
        device_id=where,
        device_id_type=MESH,
    )


def arrived(ref, sem):
    pltpu.make_async_copy(ref, ref, sem).wait()


TURNS = (1, 3, 2)


def mixer_kernel(
    x_ref,
    z_ref,
    b_ref,
    c_ref,
    fold_ref,
    act_ref,
    out_weight_ref,
    rate_ref,
    bias_ref,
    skip_ref,
    gain_ref,
    length_ref,
    state_ref,
    out_ref,
    pack,
    act,
    landed,
    weights,
    step_weights,
    keep,
    give,
    got,
    rounded,
    shared,
    shared_got,
    xz,
    bc,
    step_give,
    step_got,
    state,
    read,
    quarter,
    out_weights,
    hid,
    out_keep,
    out_give,
    out_got,
    back,
    ours,
    theirs_in,
    s_sem,
    g_send,
    g_recv,
    a_send,
    a_recv,
    b_send,
    b_recv,
    z_send,
    z_recv,
    x_send,
    x_recv,
    d_send,
    d_recv,
    r_send,
    r_recv,
    c_send,
    c_recv,
    t_sem,
    q_sem,
    w_sem,
    o_send,
    o_recv,
    h_send,
    h_recv,
    e_send,
    e_recv,
    f_send,
    f_recv,
):
    x, y, z, core = here()
    x_lo, x_hi = x % 2, x // 2
    mine = x_lo * 4 + z
    twin = device(x, y, z, core + 1)
    started = []

    target_x = x_lo * 2 + x_hi
    stays = target_x == x

    barrier = pltpu.get_barrier_semaphore()

    def signal(where):
        pl.semaphore_signal(barrier, inc=1, device_id=where, device_id_type=MESH)

    plane = [(dx, dz) for dz in (2, 1, 3, 0) for dx in (2, 1, 3, 0)]
    for dx, dz in plane[:-1]:
        signal(device(x + dx, y, z + dz, core))
    for step in TURNS:
        signal(device(x, y + step, z, core))
    signal(twin)
    pl.when(jnp.logical_not(stays))(lambda: signal(device(target_x, y, z, core)))

    fold = jnp.concatenate([fold_ref[:16], fold_ref[16:]], axis=1)
    for hi in range(2):
        for j in range(8):
            to = hi * 8 + j
            for half in range(2):
                lanes = slice((hi * 16 + half * 8 + j) * 128, (hi * 16 + half * 8 + j + 1) * 128)
                pack[to, half * 64 : half * 64 + 32] = x_ref[:, lanes]
                pack[to, half * 64 + 32 : half * 64 + 64] = z_ref[:, lanes]
            lanes = slice((hi * 4 + j % 4) * 128, (hi * 4 + j % 4 + 1) * 128)
            pack[to, 128:160] = (b_ref if j < 4 else c_ref)[:, lanes]
            pack[to, 160:176] = fold
    for hi in range(2):
        quarter[core, :, hi * 1024 : hi * 1024 + 1024] = out_weight_ref[
            :, pl.ds(pl.multiple_of((hi * 2 + core) * 1024, 1024), 1024)
        ]

    pl.semaphore_wait(barrier, 20 - jnp.where(stays, 1, 0))

    parts = (pl.ds(0, 96), pl.ds(96, 80))
    landing = landed.at[y, x_lo * 8 + z * 2 + x_hi]
    for p in range(2):
        for n, (dx, dz) in enumerate(plane):
            xd, zd = (x + dx) % 4, (z + dz) % 4
            tile = pack.at[(xd // 2) * 8 + (xd % 2) * 4 + zd, parts[p]]
            to = landing.at[parts[p]]
            if n == 15:
                pltpu.make_async_copy(tile, to, a_recv.at[p]).start()
            else:
                copy = remote(tile, to, a_send.at[p, n], a_recv.at[p], device(xd, y, zd, core))
                copy.start()
                started.append(copy)

    lane = lax.broadcasted_iota(jnp.int32, (256, 128), 1)
    from_lane = lax.broadcasted_iota(jnp.int32, (256, 128), 0)
    chosen = from_lane == (lane // 32) * 64 + core * 32 + lane % 32
    picker = jnp.where(chosen, 1.0, 0.0).astype(jnp.bfloat16)
    for i in range(16):
        spot = ((i % 8) // 2) * 4 + (i // 8) * 2 + i % 2
        act[mine, :, spot * 128 : spot * 128 + 128] = jnp.dot(
            act_ref[:, i * 256 : i * 256 + 256], picker, preferred_element_type=jnp.float32
        ).astype(jnp.bfloat16)

    def piece(dz, h):
        return act.at[x_lo * 4 + (z + dz) % 4, pl.ds(h * 64, 64)]

    def other(dz, h):
        return act.at[(1 - x_lo) * 4 + (z + dz) % 4, pl.ds(h * 64, 64)]

    def z_go(dz, h, slot, step, ref=piece):
        copy = remote(
            ref(dz, h),
            ref(dz, h),
            z_send.at[slot],
            z_recv.at[slot],
            device(x, y, z + step, core),
        )
        copy.start()
        started.append(copy)

    def x_go(dz, h, rel):
        slot = rel * 2 + h
        copy = remote(
            piece(dz, h),
            piece(dz, h),
            x_send.at[slot],
            x_recv.at[slot],
            device(x + (1 if h == 0 else 3), y, z, core),
        )
        copy.start()
        started.append(copy)

    z_go(0, 0, 0, 1)
    z_go(0, 1, 3, 3)
    x_go(0, 0, 0)
    x_go(0, 1, 0)
    z_go(0, 1, 1, 1)
    z_go(0, 0, 2, 3)

    for hi in range(2):
        copy = remote(
            out_weight_ref.at[:, pl.ds(pl.multiple_of((hi * 2 + 1 - core) * 1024, 1024), 1024)],
            quarter.at[core, :, pl.ds(hi * 1024, 1024)],
            q_sem.at[hi],
            q_sem.at[2 + hi],
            twin,
        )
        copy.start()
        started.append(copy)

    state_copies = [
        pltpu.make_async_copy(
            state_ref.at[pl.ds(n * 8, 8)], state.at[pl.ds(n * 8, 8)], s_sem.at[n]
        )
        for n in range(4)
    ]
    for copy in state_copies:
        copy.start()

    def block(dy, h, p):
        return landed.at[(y + dy) % 4, pl.ds(h * 8, 8), parts[p]]

    def y_go(dy, h, p, slot, step):
        copy = remote(
            block(dy, h, p),
            block(dy, h, p),
            b_send.at[p, slot],
            b_recv.at[p, slot],
            device(x, y + step, z, core),
        )
        copy.start()
        started.append(copy)

    def y_forward(p):
        arrived(block(3, 0, p), b_recv.at[p, 0])
        y_go(3, 0, p, 4, 1)
        arrived(block(1, 1, p), b_recv.at[p, 3])
        y_go(1, 1, p, 5, 3)

    def lay_out(dy):
        at = (y + dy) % 4
        rows = pl.ds(pl.multiple_of(at * 512, 512), 512)
        for n in range(5):
            weights[rows, n * 128 : n * 128 + 128] = landed[
                at, :, n * 32 : n * 32 + 32, :
            ].reshape(512, 128)
        pairs = landed[at, :, 160:176, :]
        step_weights[rows, :] = jnp.concatenate(
            [pairs[:, :, :64], pairs[:, :, 64:]], axis=1
        ).reshape(512, 64)

    def columns(dk, dz, h):
        k = (y + dk) % 4
        return out_weights.at[k // 2, k % 2, (z + dz) % 4, h]

    def along(h, stage):
        return (h == 1) == (stage == 1)

    def unit(h, stage, unit_at, away):
        if along(h, stage):
            return columns(away, unit_at, h)
        return columns(unit_at, away, h)

    def o_go(h, stage, unit_at, away, slot, step, part=None):
        held = unit(h, stage, unit_at, away)
        if part is not None:
            held = held.at[pl.ds(part * 16, 16)]
        where = device(x, y + step, z, core) if along(h, stage) else device(x, y, z + step, core)
        index = (stage - 1) * 8 + unit_at * (stage - 1) * 4 + h * (4 if stage == 1 else 16) + slot
        copy = remote(held, held, o_send.at[index], o_recv.at[index], where)
        copy.start()
        started.append(copy)

    def o_wait(h, stage, unit_at, away, slot, part=None):
        held = unit(h, stage, unit_at, away)
        if part is not None:
            held = held.at[pl.ds(part * 16, 16)]
        index = (stage - 1) * 8 + unit_at * (stage - 1) * 4 + h * (4 if stage == 1 else 16) + slot
        arrived(held, o_recv.at[index])

    def o_both(h, stage, unit_at):
        o_go(h, stage, unit_at, 0, 0, 1)
        o_go(h, stage, unit_at, 0, 1, 3)

    def o_forward(h, stage, unit_at):
        o_wait(h, stage, unit_at, 3, 0)
        o_go(h, stage, unit_at, 3, 2, 1, 0)
        o_wait(h, stage, unit_at, 1, 1)
        o_go(h, stage, unit_at, 1, 3, 3, 1)

    def o_last(h, stage, unit_at):
        o_wait(h, stage, unit_at, 2, 2, 0)
        o_wait(h, stage, unit_at, 2, 3, 1)

    def o_begin():
        arrived(out_weights.at[y // 2, y % 2, z], w_sem.at[1])
        for h in range(2):
            o_both(h, 1, 0)
        for h in range(2):
            o_both(h, 2, 0)

    def o_second():
        for h in range(2):
            o_forward(h, 1, 0)
            o_both(h, 2, 3)
            o_both(h, 2, 1)

    def o_third():
        for h in range(2):
            o_last(h, 1, 0)
            o_both(h, 2, 2)
        for h in range(2):
            o_forward(h, 2, 0)

    def o_fourth():
        for h in range(2):
            o_forward(h, 2, 3)
            o_forward(h, 2, 1)

    def o_fifth():
        for h in range(2):
            o_forward(h, 2, 2)

    def o_end():
        for h in range(2):
            for unit_at in range(4):
                o_last(h, 2, unit_at)

    for p in range(2):
        arrived(landed.at[y, :, parts[p]], a_recv.at[p])
        y_go(0, 0, p, 0, 1)
        y_go(0, 1, p, 3, 3)
        y_go(0, 1, p, 1, 1)
        y_go(0, 0, p, 2, 3)

    for hi in range(2):
        arrived(quarter.at[1 - core, :, pl.ds(hi * 1024, 1024)], q_sem.at[2 + hi])
    sent_on = remote(
        quarter,
        out_weights.at[y // 2, y % 2, z],
        w_sem.at[0],
        w_sem.at[1],
        device(target_x, y, z, core),
    )
    kept = pltpu.make_async_copy(quarter, out_weights.at[y // 2, y % 2, z], w_sem.at[1])
    pl.when(jnp.logical_not(stays))(sent_on.start)
    pl.when(stays)(kept.start)

    arrived(piece(3, 0), z_recv.at[0])
    z_go(3, 0, 4, 1)
    x_go(3, 0, 1)
    arrived(piece(1, 1), z_recv.at[3])
    z_go(1, 1, 5, 3)
    x_go(1, 1, 2)
    y_forward(0)
    arrived(piece(3, 1), z_recv.at[1])
    x_go(3, 1, 1)
    arrived(piece(1, 0), z_recv.at[2])
    x_go(1, 0, 2)
    lay_out(0)
    arrived(other(3, 0), x_recv.at[2])
    z_go(3, 0, 6, 1, other)
    arrived(other(1, 1), x_recv.at[5])
    z_go(1, 1, 7, 3, other)
    y_forward(1)
    o_begin()

    arrived(block(3, 1, 0), b_recv.at[0, 1])
    arrived(block(3, 1, 1), b_recv.at[1, 1])
    lay_out(3)
    arrived(block(1, 0, 0), b_recv.at[0, 2])
    arrived(block(1, 0, 1), b_recv.at[1, 2])
    lay_out(1)
    arrived(piece(2, 0), z_recv.at[4])
    arrived(piece(2, 1), z_recv.at[5])
    arrived(other(0, 0), x_recv.at[0])
    arrived(other(0, 1), x_recv.at[1])
    arrived(other(3, 1), x_recv.at[3])
    arrived(other(1, 0), x_recv.at[4])

    for p in range(2):
        arrived(block(2, 0, p), b_recv.at[p, 4])
        arrived(block(2, 1, p), b_recv.at[p, 5])
    lay_out(2)
    arrived(other(2, 0), z_recv.at[6])
    arrived(other(2, 1), z_recv.at[7])

    def to_twin(i):
        return remote(give.at[i], got.at[i], d_send.at[i], d_recv.at[i], twin)

    step_half = jnp.dot(act[mine], step_weights[...], preferred_element_type=jnp.float32)
    step_give[...] = jnp.concatenate([step_half, step_half], axis=1)
    step_copy = remote(step_give, step_got, t_sem.at[0], t_sem.at[1], twin)
    step_copy.start()

    bc_slot = x_lo * 2 + z % 2
    has_bc = core == z // 2

    def bc_twin(i):
        two = pl.ds(i * 2, 2)
        return remote(shared.at[two], shared_got.at[two], g_send.at[i], g_recv.at[i], twin)

    def multiply_bc(i, carry):
        two = pl.ds(i * 2, 2)
        shared[two] = jnp.dot(
            act[two].reshape(256, 2048), weights[:, 512:], preferred_element_type=jnp.float32
        ).reshape(2, 128, 128)
        pl.when(jnp.logical_not(has_bc))(bc_twin(i).start)
        return carry

    lax.fori_loop(0, 4, multiply_bc, 0)
    o_second()

    def multiply(turn, carry):
        i = (mine + 1 + turn) % 8
        product = jnp.dot(act[i], weights[:, :512], preferred_element_type=jnp.float32)
        first, second = product[:, :256], product[:, 256:]
        keep[i] = jnp.where(core == 0, first, second)
        give[i] = jnp.where(core == 0, second, first)
        to_twin(i).start()
        return carry

    def owner(i):
        return device(x_hi * 2 + i // 4, y, i % 4, core)

    def xz_far(i):
        return remote(rounded.at[i], xz.at[mine], r_send.at[i], r_recv.at[mine], owner(i))

    def bc_far(i):
        return remote(shared.at[i], bc.at[bc_slot], c_send.at[i], c_recv.at[bc_slot], owner(i))

    lax.fori_loop(0, 4, multiply, 0)

    @pl.when(has_bc)
    def _():
        for i in range(4):
            two = pl.ds(i * 2, 2)
            bc_twin(i).wait_recv()
            shared[two] = shared[two] + shared_got[two]

        def hand_out_bc(turn, carry):
            i = (mine + 1 + turn) % 8
            pl.when(i != mine)(lambda: bc_far(i).start())

            @pl.when(i == mine)
            def _():
                pltpu.make_async_copy(
                    shared.at[i], bc.at[bc_slot], c_recv.at[bc_slot]
                ).start()

            return carry

        lax.fori_loop(0, 8, hand_out_bc, 0)

    lax.fori_loop(4, 8, multiply, 0)
    o_third()

    def hand_out(turn, carry):
        i = (mine + 1 + turn) % 8
        to_twin(i).wait_recv()
        total = keep[i] + got[i]
        gate = total[:, 128:]
        rounded[i, :, :128] = total[:, :128].astype(jnp.bfloat16)
        rounded[i, :, 128:] = (gate / (1.0 + jnp.exp(-gate))).astype(jnp.bfloat16)
        pl.when(i != mine)(lambda: xz_far(i).start())

        @pl.when(i == mine)
        def _():
            pltpu.make_async_copy(rounded.at[i], xz.at[mine], r_recv.at[mine]).start()

        return carry

    lax.fori_loop(0, 8, hand_out, 0)
    o_fourth()

    step_copy.wait()
    step_sum = step_give[...] + step_got[...]
    step_raw = jnp.zeros((128, 16), jnp.float32)
    for t in range(4):
        step_raw += jnp.where(x_hi * 2 + core == t, step_sum[:, t * 16 : t * 16 + 16], 0.0)
    raw = step_raw + bias_ref[...]
    step_size = jnp.maximum(raw, 0.0) + jnp.log1p(jnp.exp(-jnp.abs(raw)))
    decay = jnp.exp(-jnp.exp(rate_ref[...]) * step_size)

    for slot in range(4):
        arrived(bc.at[slot], c_recv.at[slot])
    for copy in state_copies:
        copy.wait()

    def look(row, carry):
        steps_of = pl.ds(row, 4, stride=32)
        c_rows = jnp.concatenate([bc[2, steps_of, :], bc[3, steps_of, :]], axis=1)
        upper = c_rows.astype(jnp.bfloat16)
        lower = (c_rows - upper.astype(jnp.float32)).astype(jnp.bfloat16)
        seen = lax.dot_general(
            jnp.concatenate([upper, lower], axis=0),
            state[row],
            (((1,), (1,)), ((), ())),
            preferred_element_type=jnp.float32,
        )
        for t in range(4):
            read[pl.ds(t * 32 + row, 1), :] = seen[t : t + 1] + seen[t + 4 : t + 5]
        return carry

    lax.fori_loop(0, 16, look, 0, unroll=4)
    o_fifth()
    lax.fori_loop(16, 32, look, 0, unroll=4)

    at = [slice(t * 32, t * 32 + 32) for t in range(4)]
    b = jnp.concatenate([bc[0], bc[1]], axis=1)
    c = jnp.concatenate([bc[2], bc[3]], axis=1)
    rows, total, coefs = [], None, []
    for t in range(4):
        total = decay[at[t]] if t == 0 else total * decay[at[t]]
        coefs = [member * decay[at[t]] for member in coefs] + [step_size[at[t]]]
        rows.append(total)
        for s in range(t + 1):
            term = coefs[s] * jnp.sum(b[at[s]] * c[at[t]], axis=1, keepdims=True)
            rows.append(term + skip_ref[...] if s == t else term)
    table = jnp.concatenate(rows, axis=0)
    head = lax.broadcasted_iota(jnp.int32, (16, 1024), 0)
    channel = lax.broadcasted_iota(jnp.int32, (16, 1024), 1)
    spread = jnp.where(channel // 64 == head, 1.0, 0.0).astype(jnp.float32)
    wide = jnp.dot(
        table, spread, precision=lax.Precision.HIGHEST, preferred_element_type=jnp.float32
    )

    for j in range(8):
        arrived(xz.at[j], r_recv.at[j])

    def hid_part(block, away, part=None):
        rows_of = pl.ds(block * 64, 64) if part is None else pl.ds(block * 64 + part * 32, 32)
        return hid.at[(x + away) % 4, rows_of]

    def h_go(block, away, slot, step, part=None):
        held = hid_part(block, away, part)
        copy = remote(
            held, held, h_send.at[block, slot], h_recv.at[block, slot], device(x + step, y, z, core)
        )
        copy.start()
        started.append(copy)

    def h_forward(block):
        arrived(hid_part(block, 3), h_recv.at[block, 0])
        h_go(block, 3, 2, 1, 0)
        arrived(hid_part(block, 1), h_recv.at[block, 1])
        h_go(block, 1, 3, 3, 1)

    def h_last(block):
        arrived(hid_part(block, 2, 0), h_recv.at[block, 2])
        arrived(hid_part(block, 2, 1), h_recv.at[block, 3])

    for block in range(2):
        sixteen = [slice(t * 32 + block * 16, t * 32 + block * 16 + 16) for t in range(4)]
        xs = [
            jnp.concatenate([xz[j, sixteen[t], :128] for j in range(8)], axis=1).astype(
                jnp.float32
            )
            for t in range(4)
        ]
        k = block * 16
        for t in range(4):
            seen = wide[k : k + 16] * read[sixteen[t], :]
            k += 32
            for s in range(t + 1):
                seen += wide[k : k + 16] * xs[s]
                k += 32
            gate = jnp.concatenate([xz[j, sixteen[t], 128:] for j in range(8)], axis=1)
            gated = seen * gate.astype(jnp.float32)
            inv_rms = lax.rsqrt(jnp.mean(gated * gated, axis=1, keepdims=True) + eps)
            hid[x, block * 64 + t * 16 : block * 64 + t * 16 + 16, :] = (
                gated * inv_rms * gain_ref[...]
            ).astype(jnp.bfloat16)
        h_go(block, 0, 0, 1)
        h_go(block, 0, 1, 3)

    h_forward(0)
    h_last(0)
    h_forward(1)
    o_end()

    def against(left, right):
        return lax.dot_general(
            left, right, (((1,), (1,)), ((), ())), preferred_element_type=jnp.float32
        )

    def partial(block, which):
        held = out_weights[which].reshape(512, 2048)
        rows_of = slice(block * 64, block * 64 + 64)
        product = against(hid[0:2, rows_of].reshape(128, 1024), held[:, :1024]) + against(
            hid[2:4, rows_of].reshape(128, 1024), held[:, 1024:]
        )
        return product.reshape(2, 64, 512)

    theirs = 1 - x_lo

    def out_twin(block):
        return remote(
            out_give.at[block], out_got.at[block], e_send.at[block], e_recv.at[block], twin
        )

    def back_copy(block):
        return remote(
            back.at[block],
            theirs_in.at[:, pl.ds(block * 16, 16)],
            f_send.at[block],
            f_recv.at[block],
            device(x_hi * 2 + theirs, y, z, core),
        )

    def give_out(block):
        out_give[block] = partial(block, 1 - core)
        out_twin(block).start()

    def join(block):
        out_twin(block).wait_recv()
        back[block] = (out_keep[block, theirs] + out_got[block, theirs]).reshape(4, 16, 512)
        back_copy(block).start()
        ours[:, block * 16 : block * 16 + 16] = (
            out_keep[block, x_lo] + out_got[block, x_lo]
        ).reshape(4, 16, 512)

    give_out(0)
    out_keep[0] = partial(0, core)
    h_last(1)
    give_out(1)
    join(0)
    out_keep[1] = partial(1, core)
    join(1)

    for copy in started:
        copy.wait_send()
    pl.when(jnp.logical_not(stays))(sent_on.wait_send)

    def sent(i, carry):
        to_twin(i).wait_send()

        @pl.when(i != mine)
        def _():
            xz_far(i).wait_send()
            pl.when(has_bc)(bc_far(i).wait_send)

        return carry

    lax.fori_loop(0, 8, sent, 0)

    @pl.when(jnp.logical_not(has_bc))
    def _():
        for i in range(4):
            bc_twin(i).wait_send()

    for block in range(2):
        out_twin(block).wait_send()
        back_copy(block).wait_send()
        rows_of = pl.ds(block * 16, 16)
        arrived(theirs_in.at[:, rows_of], f_recv.at[block])
        first = jnp.where(x_lo == 0, ours[:, rows_of], theirs_in[:, rows_of])
        second = jnp.where(x_lo == 0, theirs_in[:, rows_of], ours[:, rows_of])
        for j in range(8):
            span = slice(j * 64, j * 64 + 64)
            mix = jnp.concatenate([first[:, :, span], second[:, :, span]], axis=2)
            lanes = pl.ds(pl.multiple_of((x_hi * 2 + core) * 1024 + j * 128, 128), 128)
            for t in range(4):
                residual = act_ref[t * 32 + block * 16 : t * 32 + block * 16 + 16, lanes].astype(
                    jnp.float32
                )
                active = length_ref[block * 16 : block * 16 + 16] > t
                out_ref[t, rows_of, j * 128 : j * 128 + 128] = jnp.where(
                    active, residual + mix[t], residual
                ).astype(jnp.bfloat16)


def mixer(weight_x, weight_z, weight_b, weight_c, weight_step, flat_in, out_weight, log_rate, step_bias, skip_gain, norm_gain, lengths, state):
    dma = pltpu.SemaphoreType.DMA
    vmem = pl.BlockSpec(memory_space=pltpu.VMEM)
    bf16, f32 = jnp.bfloat16, jnp.float32
    return pl.pallas_call(
        mixer_kernel,
        out_shape=jax.ShapeDtypeStruct((4, 32, 1024), bf16),
        in_specs=[vmem] * 12 + [pl.BlockSpec(memory_space=pl.ANY)],
        out_specs=vmem,
        scratch_shapes=[
            pltpu.VMEM((16, 176, 128), bf16),
            pltpu.VMEM((8, 128, 2048), bf16),
            pltpu.VMEM((4, 16, 176, 128), bf16),
            pltpu.VMEM((2048, 640), bf16),
            pltpu.VMEM((2048, 64), bf16),
            pltpu.VMEM((8, 128, 256), f32),
            pltpu.VMEM((8, 128, 256), f32),
            pltpu.VMEM((8, 128, 256), f32),
            pltpu.VMEM((8, 128, 256), bf16),
            pltpu.VMEM((8, 128, 128), f32),
            pltpu.VMEM((8, 128, 128), f32),
            pltpu.VMEM((8, 128, 256), bf16),
            pltpu.VMEM((4, 128, 128), f32),
            pltpu.VMEM((128, 128), f32),
            pltpu.VMEM((128, 128), f32),
            pltpu.VMEM((32, 1024, 256), bf16),
            pltpu.VMEM((128, 1024), f32),
            pltpu.VMEM((2, 32, 2048), bf16),
            pltpu.VMEM((2, 2, 4, 2, 32, 2048), bf16),
            pltpu.VMEM((4, 128, 1024), bf16),
            pltpu.VMEM((2, 2, 64, 512), f32),
            pltpu.VMEM((2, 2, 64, 512), f32),
            pltpu.VMEM((2, 2, 64, 512), f32),
            pltpu.VMEM((2, 4, 16, 512), f32),
            pltpu.VMEM((4, 32, 512), f32),
            pltpu.VMEM((4, 32, 512), f32),
            dma((4,)),
            dma((4,)),
            dma((4,)),
            dma((2, 15)),
            dma((2,)),
            dma((2, 6)),
            dma((2, 6)),
            dma((8,)),
            dma((8,)),
            dma((6,)),
            dma((6,)),
            dma((8,)),
            dma((8,)),
            dma((8,)),
            dma((8,)),
            dma((8,)),
            dma((4,)),
            dma((2,)),
            dma((4,)),
            dma((2,)),
            dma((40,)),
            dma((40,)),
            dma((2, 4)),
            dma((2, 4)),
            dma((2,)),
            dma((2,)),
            dma((2,)),
            dma((2,)),
        ],
        compiler_params=pltpu.CompilerParams(
            collective_id=0, has_side_effects=True, vmem_limit_bytes=58 << 20
        ),
        cost_estimate=pl.CostEstimate(
            flops=4 << 30, bytes_accessed=200 << 20, transcendentals=0
        ),
        name="mixer",
    )(
        weight_x,
        weight_z,
        weight_b,
        weight_c,
        weight_step,
        flat_in,
        out_weight,
        log_rate.reshape(1, 16),
        step_bias.reshape(1, 16),
        skip_gain.reshape(1, 16),
        norm_gain.reshape(1, 1024),
        lengths.reshape(32, 1),
        state,
    )


def shards(
    layer_in,
    lengths,
    prior_state,
    weight_x,
    weight_z,
    weight_b,
    weight_c,
    weight_step,
    weight_out,
    log_rate,
    step_bias,
    skip_gain,
    norm_gain,
):
    flat_in = layer_in.reshape(128, 4096)

    return mixer(
        weight_x,
        weight_z,
        weight_b,
        weight_c,
        weight_step,
        flat_in,
        weight_out.T,
        log_rate,
        step_bias,
        skip_gain,
        norm_gain,
        lengths,
        prior_state.reshape(32, 1024, 256),
    )


def solution(mesh):
    placed = (
        P(None, "group", None),
        P("group"),
        P("group", "tensor", None, None),
        P(("group", "tensor"), None),
        P(("group", "tensor"), None),
        P(("group", "tensor"), None),
        P(("group", "tensor"), None),
        P(("group", "tensor"), None),
        P(None, ("group", "tensor")),
        P("tensor"),
        P("tensor"),
        P("tensor"),
        P("tensor"),
    )
    return jax.shard_map(
        shards, mesh=mesh, in_specs=placed, out_specs=P(None, "group", "tensor"), check_vma=False
    )
```
